256 devices in a mesh: gx: 64 (over z, y, core), gy: 4 (over x).
Axes of the slice: x: 4, y: 4, z: 8, core: 2. Of those that a mesh axis runs over, the one named last changes fastest.
Arguments:
- latent: float32 [512, 32, 4, 256], P('gx', 'gy'), may hold values from -6 to 6
- active: int32 [128, 8, 1], P('gx', 'gy'), may hold values from 0 to 1, as said below
- parent_owner: int32 [64, 4, 4, 4], P('gx', 'gy'), may hold values from 0 to 63, all different within a row; in each aligned block of 4 rows (0 to 3, 4 to 7, ..., all dimensions but the last counted through in order) at most 2 rows name the same one
- parent_slot: int32 [64, 4, 4, 4], P('gx', 'gy'), may hold values from 0 to 3
- coarse_kv: bfloat16 [256, 128, 512], P('gx')
- norm_gain: float32 [256], replicated, may hold values from 0.5 to 1.5
- conv_weight: bfloat16 [27, 256, 256], replicated, may hold values from -0.078125 to 0.078125
- conv_bias: float32 [256], replicated, may hold values from -3 to 3
- attn_gain: float32 [256], replicated, may hold values from 0.1 to 1.9
- q_weight: bfloat16 [256, 256], replicated, may hold values from -0.375 to 0.375
- out_weight: bfloat16 [256, 256], replicated, may hold values from -1.5 to 1.5
Outputs:
- denoised: float32 [512, 32, 4, 256], P('gx', 'gy')
The draws below stay inside these ranges and needn't reach their ends.
Inputs may be any that keep to these rules, and one draw needn't show every extreme that they name: `active`: active blocks of one device: at least one eighth of 4, and never fewer than one; at most 3, and some device has exactly 3. `parent_owner`: the 4 owners of one window are distinct; among the windows of one device no owner is named by more than 2 windows, and some device names some owner exactly 2 times.
All inputs are finite; a program needn't handle non-finite values.
Results may differ from the reference program's by a relative error of at most 0.03.
The reference program's roundings to bfloat16 on the way (of `normed`, `query_in`, `queries`, `weights` and `attended`) count: a program that leaves them out, or rounds other values in their place, can miss the bound.
Values may be sent and summed in bfloat16 or wider, within the bound.
No kernel may reach another device: no remote copies, remote signals or barrier semaphores. Data moves between devices by JAX's collectives and lax.ppermute only.
A program may use at most 128 MiB of HBM per device.

```python
import math
import jax
import jax.numpy as jnp
import numpy as np
from jax import lax

CH = 256
HEADS = 8
EDGE = 4
BX = 2
BY = 2
BZ = 1
WIN_DEV = 4
ACT_MAX = 3
PARENTS = 4
COARSE_TOK = 128
SLOTS = 2
REG_DEV = 4
REGIONS = 256
NVX = 512
NVY = 32
NVZ = 4
N_GX = 64
N_GY = 4


def draw_active(key, part):
    key = jax.random.fold_in(key, 11)
    devices = N_GX * N_GY
    lowest = max(1, WIN_DEV // 8)
    first_key, second_key, third_key = jax.random.split(key, 3)
    counts = jax.random.randint(first_key, (devices,), lowest, ACT_MAX + 1)
    busiest = jax.random.randint(second_key, (), 0, devices)
    counts = counts.at[busiest].set(ACT_MAX)
    ranking = jax.vmap(lambda one_key: jax.random.permutation(one_key, WIN_DEV))(jax.random.split(third_key, devices))
    flags = (ranking < counts[:, None]).astype(jnp.int32)
    flags = flags.reshape(N_GX, N_GY, BX, BY, BZ).transpose(0, 2, 1, 3, 4)
    return flags.reshape(N_GX * BX, N_GY * BY, BZ)


def draw_coarse_kv(key, part):
    key = jax.random.fold_in(key, 5)
    shape = (REGIONS, COARSE_TOK, 2 * CH)
    result = jax.random.normal(key, shape, jnp.float32)
    return result.astype(jnp.bfloat16)


def place_ends(drawn, key, least, largest):
    spot = [jax.random.randint(jax.random.fold_in(key, axis), (), 0, length) for axis, length in enumerate(drawn.shape)]
    widest = drawn.shape.index(max(drawn.shape))
    beside = spot[:widest] + [(spot[widest] + 1) % drawn.shape[widest]] + spot[widest + 1:]
    return drawn.at[tuple(spot)].set(least).at[tuple(beside)].set(largest)


def block_scale(stream_key, dims, shards, least, largest):
    factor_of = 1.0
    for position, shards_of in shards:
        heights = jax.random.uniform(jax.random.fold_in(jax.random.fold_in(stream_key, 6), position), (shards_of,), jnp.float32, least / len(shards), largest / len(shards))
        factor_of = factor_of * jnp.repeat(jnp.exp(heights), dims[position] // shards_of).reshape((-1,) + (1,) * (len(dims) - 1 - position))
    return factor_of


def assign_block(key, own, number, rows, number_of, top, reach, skew):
    order = jax.random.permutation(key, number_of)
    packed, common = shares(number_of, rows * top, reach, skew, True), shares(number_of, rows * top, reach, skew, False)
    places = jnp.arange(number_of)

    def named(tallies, offset_by):
        used = int((tallies > 0).sum())
        fixed = max(1, used // 4)
        moved = fixed + (places - fixed + offset_by * (used - fixed)) % max(1, number_of - fixed)
        return jnp.zeros((number_of,), jnp.int32).at[order[jnp.where(places < fixed, places, moved)]].set(jnp.asarray(tallies, jnp.int32))

    tallies = jnp.where(number % 4 == 0, named(packed, number // 4), named(common, number - number // 4 - 1))
    mixed = jax.random.permutation(jax.random.fold_in(own, 3), number_of)
    donor, receiver = mixed[0:number_of // 2 * 2:2], mixed[1:number_of // 2 * 2:2]
    room = jnp.minimum(tallies[donor] - 1, reach - tallies[receiver]) // 2
    room = jnp.where((donor == order[0]) | (receiver == order[0]) | (tallies[receiver] == 0), 0, jnp.maximum(room, 0))
    moved = jax.random.randint(jax.random.fold_in(own, 4), (number_of // 2,), 0, 1 << 20) % (room + 1)
    tallies = tallies.at[donor].add(-moved).at[receiver].add(moved)
    items = jnp.searchsorted(jnp.cumsum(tallies), jnp.arange(rows * top), side="right").astype(jnp.int32)
    listing = items.reshape(top, rows).T
    listing = listing[jax.random.permutation(jax.random.fold_in(own, 1), rows)]
    offset_by = jax.random.randint(jax.random.fold_in(own, 2), (rows, 1), 0, top)
    return jnp.take_along_axis(listing, (jnp.arange(top)[None, :] + offset_by) % top, axis=1)


def shares(count, total, bound, lean, full):
    portions = [(1 << 20) // math.isqrt(rank ** lean) + 1 for rank in range(1, count + 1)]
    largest = bound if full else min(bound, max(-(-total // count), total * portions[0] // sum(portions)))
    least = 1 if total - largest >= count - 1 else 0
    holding, spare = [largest] + [least] * (count - 1), total - largest - least * (count - 1)
    while spare > 0:
        free = [i for i in range(1, count) if holding[i] < largest] or [i for i in range(1, count) if holding[i] < bound]
        whole, left = sum([portions[i] for i in free]), spare
        for i in free:
            extra = min(bound - holding[i], max(1, left * portions[i] // whole), spare)
            holding[i] = holding[i] + extra
            spare = spare - extra
    return np.array(holding)


def bell_draw(stream_key, shape, scale, bound, shards=(), kind=jnp.bfloat16):
    array = jax.random.normal(stream_key, shape, jnp.float32) * scale
    if len(shards) > 0:
        array = block_scale(stream_key, shape, shards, -0.22, 0.18) * array
    return jnp.clip(array, min=-bound, max=bound).astype(kind)


def setup_inputs(seed: int = 0) -> dict:
    seeds = jax.random.split(jax.random.key(seed), 12)
    latent = bell_draw(seeds[0], (NVX, NVY, NVZ, CH), 1.0, 6.0, ((0, 64), (1, 4)), jnp.float32)
    active = draw_active(jax.random.fold_in(seeds[11], 71), 0)
    parent_owner_keys = jax.random.split(jax.random.fold_in(seeds[2], 1), N_GX * N_GY * WIN_DEV // WIN_DEV)
    parent_owner_turns = jax.random.permutation(jax.random.fold_in(seeds[2], 3), N_GX * N_GY * WIN_DEV // WIN_DEV)
    parent_owner = jax.vmap(lambda own, number: assign_block(jax.random.fold_in(seeds[2], 2), own, number, WIN_DEV, N_GX, PARENTS, SLOTS, 0))(parent_owner_keys, parent_owner_turns).reshape((N_GX, N_GY, WIN_DEV, PARENTS))
    parent_slot = place_ends(jax.random.randint(seeds[3], (N_GX, N_GY, WIN_DEV, PARENTS), 0, REG_DEV), jax.random.fold_in(seeds[3], 1), 0, REG_DEV - 1).astype(jnp.int32)
    coarse_kv = draw_coarse_kv(jax.random.fold_in(seeds[11], 71), 0)
    norm_gain = jnp.clip(1.0 + 0.1 * jax.random.normal(seeds[5], (CH,), jnp.float32), 0.5, 1.5)
    conv_weight = bell_draw(seeds[6], (27, CH, CH), (27 * CH) ** -0.5, 0.078125)
    conv_bias = bell_draw(seeds[7], (CH,), 0.5, 3.0, (), jnp.float32)
    attn_gain = jnp.clip(1.0 + 0.18 * jax.random.normal(seeds[8], (CH,), jnp.float32), 0.1, 1.9)
    q_weight = bell_draw(seeds[9], (CH, CH), CH ** -0.5, 0.375)
    out_weight = bell_draw(seeds[10], (CH, CH), (CH // 16) ** -0.5, 1.5)
    return {"latent": latent, "active": active, "parent_owner": parent_owner, "parent_slot": parent_slot, "coarse_kv": coarse_kv, "norm_gain": norm_gain, "conv_weight": conv_weight, "conv_bias": conv_bias, "attn_gain": attn_gain, "q_weight": q_weight, "out_weight": out_weight}


def rms_scale(values):
    return lax.rsqrt(lax.optimization_barrier(jnp.mean(values * values, axis=-1, keepdims=True)) + 1e-06)

def reference(latent, active, parent_owner, parent_slot, coarse_kv, norm_gain, conv_weight, conv_bias, attn_gain, q_weight, out_weight):
    head_dim = CH // HEADS
    voxel_mask = jnp.repeat(jnp.repeat(jnp.repeat(active.astype(jnp.float32), EDGE, 0), EDGE, 1), EDGE, 2)[..., None]
    normed = (voxel_mask * latent * rms_scale(latent) * norm_gain).astype(jnp.bfloat16)
    padded = jnp.pad(normed, ((1, 1), (1, 1), (1, 1), (0, 0)))
    size_x, size_y, size_z = (latent.shape[0], latent.shape[1], latent.shape[2])
    conv_sum = jnp.zeros((size_x * size_y * size_z, CH), jnp.float32)
    for offset in range(27):
        shift_x, shift_y, shift_z = (offset // 9, offset // 3 % 3, offset % 3)
        shifted = padded[shift_x:shift_x + size_x, shift_y:shift_y + size_y, shift_z:shift_z + size_z].reshape(-1, CH)
        conv_sum = conv_sum + jnp.dot(shifted, conv_weight[offset], preferred_element_type=jnp.float32)
    conv_sum = conv_sum.reshape(size_x, size_y, size_z, CH) + conv_bias
    hidden = latent + voxel_mask * jax.nn.silu(conv_sum)
    query_in = (hidden * rms_scale(hidden) * attn_gain).astype(jnp.bfloat16)
    queries = jnp.dot(query_in.reshape(-1, CH), q_weight, preferred_element_type=jnp.float32).astype(jnp.bfloat16)
    slab_queries = queries.reshape(N_GX, BX, EDGE, N_GY, BY, EDGE, BZ, EDGE, CH)
    slab_queries = slab_queries.transpose(0, 3, 1, 4, 6, 2, 5, 7, 8).reshape(N_GX, N_GY * BX * BY * BZ, EDGE ** 3, CH)
    regions = (parent_owner * REG_DEV + parent_slot).astype(jnp.int32).reshape(N_GX, N_GY * WIN_DEV, PARENTS)

    def attend_slab(bundle):
        these_queries, these_regions = bundle
        members = these_queries.shape[0]
        kv_rows = coarse_kv[these_regions].reshape(members, PARENTS * COARSE_TOK, 2 * CH).astype(jnp.float32)
        q_heads = these_queries.astype(jnp.float32).reshape(members, EDGE ** 3, HEADS, head_dim)
        k_heads = kv_rows[:, :, :CH].reshape(members, PARENTS * COARSE_TOK, HEADS, head_dim)
        v_heads = kv_rows[:, :, CH:].reshape(members, PARENTS * COARSE_TOK, HEADS, head_dim)
        scores = jnp.einsum('mqhd,mkhd->mhqk', q_heads, k_heads, precision=lax.Precision.HIGHEST) / math.sqrt(head_dim)
        weights = lax.optimization_barrier(jax.nn.softmax(scores, axis=-1).astype(jnp.bfloat16)).astype(jnp.float32)
        mixed = jnp.einsum('mhqk,mkhd->mqhd', weights, v_heads, precision=lax.Precision.HIGHEST)
        return mixed.reshape(members, EDGE ** 3, CH).astype(jnp.bfloat16)
    attended = lax.map(attend_slab, (slab_queries, regions))
    attended = attended.reshape(N_GX, N_GY, BX, BY, BZ, EDGE, EDGE, EDGE, CH)
    attended = attended.transpose(0, 2, 5, 1, 3, 6, 4, 7, 8).reshape(-1, CH)
    projected = jnp.dot(attended, out_weight, preferred_element_type=jnp.float32).reshape(size_x, size_y, size_z, CH)
    return voxel_mask * (hidden + projected)
```

```python
import math

import jax
import jax.numpy as jnp
import numpy as np
from jax import lax
from jax.experimental import pallas as pl
from jax.experimental.pallas import tpu as pltpu
from jax.sharding import PartitionSpec as P

CH = 256
HEADS = 8
HEAD_DIM = 32
EDGE = 4
VX, VY, VZ = 8, 8, 4
ROWS = VX * VY * VZ
WINDOWS = 4
ACT_MAX = 3
PARENTS = 4
TOK = 128
LANES = 128
PACK = 144
SCALE = math.log2(math.e) / math.sqrt(HEAD_DIM)
LOWEST = -3e38
F32 = jnp.float32
BF16 = jnp.bfloat16
VMEM = pl.BlockSpec(memory_space=pltpu.VMEM)
SMEM = pl.BlockSpec(memory_space=pltpu.SMEM)
ANY = pl.BlockSpec(memory_space=pl.ANY)
NT = (((1,), (1,)), ((), ()))


def placement():
    row = np.arange(ROWS)
    z, x, y = row // 64, row // 8 % 8, row % 8
    window = (x // EDGE) * 2 + y // EDGE
    query = z * 16 + x % EDGE * 4 + y % EDGE
    lane = np.arange(LANES) % 64
    hit = (window[None, :, None] == np.arange(WINDOWS)[:, None, None]) & (
        query[None, :, None] == lane[None, None, :]
    )
    return hit.astype(np.float32)


def row_mask(act_ref):
    low = lax.broadcasted_iota(jnp.int32, (VY, CH), 0) < EDGE
    flags = [act_ref[w].astype(F32) for w in range(WINDOWS)]
    halves = [jnp.where(low, flags[2 * b], flags[2 * b + 1]) for b in range(2)]
    return jnp.concatenate(
        [jnp.broadcast_to(half[None], (EDGE, VY, CH)) for half in halves], axis=0
    )


def conv_kernel(
    act_ref, slot_ref, latent_ref, xlo_ref, xhi_ref, ylo_ref, yhi_ref, ngain_ref, bias_ref,
    again_ref, weight_ref, qw_ref, place_ref, extra_ref, hidden_ref, query_ref,
    frame, weights, sems,
):
    copies = [
        pltpu.make_async_copy(weight_ref.at[pl.ds(3 * ab, 3)], weights.at[pl.ds(3 * ab, 3)], sems.at[ab])
        for ab in range(9)
    ]
    for copy in copies:
        copy.start()
    latent = latent_ref[...]
    mask = row_mask(act_ref)[None]
    scale = lax.rsqrt(jnp.mean(latent * latent, axis=-1, keepdims=True) + 1e-06)
    normed = mask * latent * scale * ngain_ref[...].reshape(1, 1, 1, CH)
    frame[1, :, 1 : VX + 1] = normed
    frame[1, :, 0] = xlo_ref[...].astype(F32)
    frame[1, :, VX + 1] = xhi_ref[...].astype(F32)
    ylo = ylo_ref[...].astype(F32)
    yhi = yhi_ref[...].astype(F32)
    first = lax.broadcasted_iota(jnp.int32, (VY, CH), 0) == 0
    last = lax.broadcasted_iota(jnp.int32, (VY, CH), 0) == VY - 1
    for z in range(VZ):
        for x in range(VX + 2):
            r = z * (VX + 2) + x
            here = frame[1, z, x]
            frame[0, z, x] = jnp.where(first, ylo[r : r + 1, :], pltpu.roll(here, 1, 0))
            frame[2, z, x] = jnp.where(last, yhi[r : r + 1, :], pltpu.roll(here, VY - 1, 0))
    mid = jnp.zeros((ROWS, CH), F32)
    up = jnp.zeros((ROWS - 64, CH), F32)
    down = jnp.zeros((ROWS - 64, CH), F32)
    for ab in range(9):
        copies[ab].wait()
        a, b = ab // 3, ab % 3
        slab = frame[b, :, a : a + VX].reshape(ROWS, CH).astype(BF16)
        up = up + jnp.dot(slab[: ROWS - 64], weights[3 * ab], preferred_element_type=F32)
        mid = mid + jnp.dot(slab, weights[3 * ab + 1], preferred_element_type=F32)
        down = down + jnp.dot(slab[64:], weights[3 * ab + 2], preferred_element_type=F32)
    gap = jnp.zeros((64, CH), F32)
    conv = mid + jnp.concatenate([gap, up], 0) + jnp.concatenate([down, gap], 0) + bias_ref[...]
    flat_mask = jnp.broadcast_to(mask, (VZ, VX, VY, CH)).reshape(ROWS, CH)
    hidden = latent.reshape(ROWS, CH) + flat_mask * (conv / (1.0 + jnp.exp(-conv)))
    hidden_ref[...] = hidden
    scale = lax.rsqrt(jnp.mean(hidden * hidden, axis=-1, keepdims=True) + 1e-06)
    query_in = (hidden * scale * again_ref[...]).astype(BF16)
    queries = lax.dot_general(qw_ref[...], query_in, NT, preferred_element_type=F32).astype(BF16)
    left = lax.broadcasted_iota(jnp.int32, (LANES, LANES), 1) < 64
    query_ref[:, :LANES, :] = jnp.zeros((ACT_MAX, LANES, LANES), BF16)
    query_ref[:, LANES:, :] = extra_ref[...]
    for w in range(WINDOWS):
        @pl.when(act_ref[w] > 0)
        def _(w=w):
            both = jnp.dot(queries, place_ref[w], preferred_element_type=F32)
            query_ref[slot_ref[w], :LANES, :] = jnp.where(left, both[:LANES], both[LANES:]).astype(BF16)


def attend_kernel(code_ref, *refs):
    query_refs, kv_ref, out_refs = refs[:4], refs[4], refs[5:9]
    held, blocks, sums, peak, total, sems = refs[9:]

    def fetch(n):
        region = jnp.maximum(code_ref[n], 0)
        return pltpu.make_async_copy(kv_ref.at[region], held.at[n], sems.at[n])

    def begin(n, carry):
        @pl.when(code_ref[n] >= 0)
        def _():
            fetch(n).start()
        return carry

    lax.fori_loop(0, 4 * ACT_MAX * PARENTS, begin, 0)
    blocks[...] = jnp.zeros_like(blocks)
    left = lax.broadcasted_iota(jnp.int32, (HEAD_DIM, LANES), 1) < 64
    for source in range(4):
        query_ref, out_ref = query_refs[source], out_refs[source]

        def window(s, carry, source=source, query_ref=query_ref, out_ref=out_ref):
            base = (source * ACT_MAX + s) * PARENTS
            found = code_ref[base]
            for p in range(1, PARENTS):
                found = jnp.maximum(found, code_ref[base + p])

            @pl.when(found < 0)
            def _():
                out_ref[s, :LANES, :] = jnp.zeros((LANES, LANES), BF16)
                rows = lax.broadcasted_iota(jnp.int32, (PACK - LANES, LANES), 0)
                out_ref[s, LANES:, :] = jnp.where(rows < 4, LOWEST, 0.0).astype(BF16)

            @pl.when(found >= 0)
            def _():
                for j in range(4):
                    pair = query_ref[s, 32 * j : 32 * j + 32, :].astype(F32)
                    lanes = slice(LANES * j, LANES * j + LANES)
                    blocks[64 * j : 64 * j + 32, lanes] = jnp.where(left, pair, 0.0).astype(BF16)
                    blocks[64 * j + 32 : 64 * j + 64, lanes] = jnp.where(left, 0.0, pair).astype(BF16)
                sums[...] = jnp.zeros_like(sums)
                peak[...] = jnp.full_like(peak, LOWEST)
                total[...] = jnp.zeros_like(total)

                def parent(p, carry):
                    n = base + p

                    @pl.when(code_ref[n] >= 0)
                    def _():
                        fetch(n).wait()
                        for g in range(2):
                            half = slice(LANES * g, LANES * g + LANES)
                            wide = slice(256 * g, 256 * g + 256)
                            scores = jnp.dot(held[n, :, half], blocks[half, wide], preferred_element_type=F32)
                            old = peak[:, wide]
                            new = jnp.maximum(old, jnp.max(scores, axis=0, keepdims=True))
                            lifted = jnp.exp2((scores - new) * SCALE)
                            fade = jnp.exp2((old - new) * SCALE)
                            peak[:, wide] = new
                            total[:, wide] = total[:, wide] * fade + jnp.sum(lifted, axis=0, keepdims=True)
                            mixed = jnp.dot(
                                held[n, :, CH + LANES * g : CH + LANES * g + LANES],
                                lifted.astype(BF16), preferred_element_type=F32,
                            )
                            for jj in range(2):
                                rows = slice(64 * (2 * g + jj), 64 * (2 * g + jj) + 64)
                                cut = slice(LANES * jj, LANES * jj + LANES)
                                sums[rows, :] = sums[rows, :] * fade[:, cut] + mixed[64 * jj : 64 * jj + 64, cut]
                    return carry

                lax.fori_loop(0, PARENTS, parent, 0)
                levels = []
                for j in range(4):
                    lanes = slice(LANES * j, LANES * j + LANES)
                    kept = jnp.where(left, sums[64 * j : 64 * j + 32, :], sums[64 * j + 32 : 64 * j + 64, :])
                    out_ref[s, 32 * j : 32 * j + 32, :] = (kept / total[:, lanes]).astype(BF16)
                    levels.append(peak[:, lanes] * SCALE + jnp.log2(total[:, lanes]))
                level = jnp.concatenate(levels, axis=0)
                high = level.astype(BF16).astype(F32)
                middle = (level - high).astype(BF16).astype(F32)
                low = level - high - middle
                stats = jnp.concatenate([high, middle, low, jnp.zeros_like(low)], axis=0)
                out_ref[s, LANES:, :] = stats.astype(BF16)
            return carry

        lax.fori_loop(0, ACT_MAX, window, 0)


def merge_kernel(act_ref, slot_ref, *refs):
    part_refs = refs[:4]
    hidden_ref, ow_ref, place_ref, out_ref, mixed, attended = refs[4:]
    for s in range(ACT_MAX):
        stats = [ref[s, LANES:, :].astype(F32) for ref in part_refs]
        levels = [one[0:4] + one[4:8] + one[8:12] for one in stats]
        top = jnp.maximum(jnp.maximum(levels[0], levels[1]), jnp.maximum(levels[2], levels[3]))
        shares = [jnp.exp2(level - top) for level in levels]
        whole = shares[0] + shares[1] + shares[2] + shares[3]
        for j in range(4):
            rows = slice(32 * j, 32 * j + 32)
            value = jnp.zeros((HEAD_DIM, LANES), F32)
            for ref, share in zip(part_refs, shares):
                value = value + ref[s, rows, :].astype(F32) * (share / whole)[j : j + 1, :]
            mixed[s, rows, :] = value.astype(BF16)
    attended[...] = jnp.zeros_like(attended)
    left = lax.broadcasted_iota(jnp.int32, (ROWS, LANES), 1) < 64
    for w in range(WINDOWS):
        @pl.when(act_ref[w] > 0)
        def _(w=w):
            block = mixed[slot_ref[w]]
            place = place_ref[w].astype(F32)
            attended[0] += lax.dot_general(
                jnp.where(left, place, 0.0).astype(BF16), block, NT, preferred_element_type=F32
            )
            attended[1] += lax.dot_general(
                jnp.where(left, 0.0, place).astype(BF16), block, NT, preferred_element_type=F32
            )
    projected = jnp.dot(attended[0].astype(BF16), ow_ref[0], preferred_element_type=F32)
    projected = projected + jnp.dot(attended[1].astype(BF16), ow_ref[1], preferred_element_type=F32)
    mask = jnp.broadcast_to(row_mask(act_ref)[None], (VZ, VX, VY, CH)).reshape(ROWS, CH)
    out_ref[...] = mask * (hidden_ref[...] + projected)


def shift(block, axis, step):
    count = lax.axis_size(axis)
    return lax.ppermute(block, axis, [(i, i + step) for i in range(count) if 0 <= i + step < count])


def turn(block, axis, step):
    count = lax.axis_size(axis)
    return lax.ppermute(block, axis, [(i, (i + step) % count) for i in range(count)])


def per_device(
    latent, active, parent_owner, parent_slot, coarse_kv, norm_gain, conv_weight, conv_bias,
    attn_gain, q_weight, out_weight,
):
    plane = lax.axis_index("gy")
    mine = lax.dynamic_index_in_dim(coarse_kv, plane, 0, keepdims=False)
    mine = jnp.concatenate([mine[:, :CH], mine[:, CH : CH + 128].T, mine[:, CH + 128 :].T], axis=1)
    kv_all = lax.all_gather(mine, "gx")

    act = active.reshape(WINDOWS)
    slots = jnp.cumsum(act) - 1
    hit = (act[None, :] > 0) & (slots[None, :] == jnp.arange(ACT_MAX)[:, None])
    codes = (parent_owner * 4 + parent_slot).reshape(WINDOWS, PARENTS) + 1
    codes = jnp.sum(jnp.where(hit[:, :, None], codes[None], 0), axis=1) - 1
    extra = jnp.zeros((ACT_MAX, PACK - LANES, LANES), BF16).at[:, 0, :PARENTS].set(codes.astype(BF16))

    turned = latent.transpose(2, 0, 1, 3)
    mask = jnp.repeat(jnp.repeat(active[:, :, 0].astype(F32), EDGE, 0), EDGE, 1)

    def normed(values, flags):
        scale = lax.rsqrt(jnp.mean(values * values, axis=-1, keepdims=True) + 1e-06)
        return (flags[None, :, None] * values * scale * norm_gain).astype(BF16)

    x_first, x_last = normed(turned[:, 0], mask[0]), normed(turned[:, -1], mask[-1])
    y_first, y_last = normed(turned[:, :, 0], mask[:, 0]), normed(turned[:, :, -1], mask[:, -1])
    x_low, x_high = shift(x_last, "gx", 1), shift(x_first, "gx", -1)
    y_first = jnp.concatenate([x_low[:, :1], y_first, x_high[:, :1]], axis=1).reshape(-1, CH)
    y_last = jnp.concatenate([x_low[:, -1:], y_last, x_high[:, -1:]], axis=1).reshape(-1, CH)
    y_low, y_high = shift(y_last, "gy", 1), shift(y_first, "gy", -1)

    place = jnp.asarray(placement(), BF16)
    qw = q_weight.reshape(CH, 4, 2, HEAD_DIM).transpose(2, 1, 3, 0).reshape(CH, CH)
    ow = out_weight.reshape(4, 2, HEAD_DIM, CH).transpose(1, 0, 2, 3).reshape(2, LANES, CH)

    hidden, query = pl.pallas_call(
        conv_kernel,
        out_shape=(
            jax.ShapeDtypeStruct((ROWS, CH), F32),
            jax.ShapeDtypeStruct((ACT_MAX, PACK, LANES), BF16),
        ),
        in_specs=[SMEM, SMEM] + [VMEM] * 8 + [ANY] + [VMEM] * 3,
        out_specs=(VMEM, VMEM),
        scratch_shapes=[
            pltpu.VMEM((3, VZ, VX + 2, VY, CH), F32),
            pltpu.VMEM((27, CH, CH), BF16),
            pltpu.SemaphoreType.DMA((9,)),
        ],
        compiler_params=pltpu.CompilerParams(vmem_limit_bytes=24 << 20),
        cost_estimate=pl.CostEstimate(flops=2 * 27 * ROWS * CH * CH, bytes_accessed=5 << 20, transcendentals=ROWS * CH),
        name="conv",
    )(
        act, slots, turned, x_low, x_high, y_low, y_high, norm_gain.reshape(1, CH),
        conv_bias.reshape(1, CH), attn_gain.reshape(1, CH), conv_weight, qw, place, extra,
    )

    queries = [query] + [turn(query, "gy", d) for d in range(1, 4)]
    wanted = jnp.concatenate([one[:, LANES, :PARENTS] for one in queries]).astype(jnp.int32).reshape(-1)
    wanted = jnp.where((wanted >= 0) & (wanted % 4 == plane), wanted // 4, -1)

    parts = pl.pallas_call(
        attend_kernel,
        out_shape=[jax.ShapeDtypeStruct((ACT_MAX, PACK, LANES), BF16)] * 4,
        in_specs=[SMEM] + [VMEM] * 4 + [ANY],
        out_specs=[VMEM] * 4,
        scratch_shapes=[
            pltpu.VMEM((4 * ACT_MAX * PARENTS, TOK, 2 * CH), BF16),
            pltpu.VMEM((CH, 2 * CH), BF16),
            pltpu.VMEM((CH, LANES), F32),
            pltpu.VMEM((1, 2 * CH), F32),
            pltpu.VMEM((1, 2 * CH), F32),
            pltpu.SemaphoreType.DMA((4 * ACT_MAX * PARENTS,)),
        ],
        compiler_params=pltpu.CompilerParams(vmem_limit_bytes=24 << 20),
        name="attend",
    )(wanted, *queries, kv_all)

    merged = [parts[0]] + [turn(parts[d], "gy", -d) for d in range(1, 4)]
    out = pl.pallas_call(
        merge_kernel,
        out_shape=jax.ShapeDtypeStruct((ROWS, CH), F32),
        in_specs=[SMEM, SMEM] + [VMEM] * 7,
        out_specs=VMEM,
        scratch_shapes=[
            pltpu.VMEM((ACT_MAX, LANES, LANES), BF16),
            pltpu.VMEM((2, ROWS, LANES), F32),
        ],
        compiler_params=pltpu.CompilerParams(vmem_limit_bytes=16 << 20),
        name="merge",
    )(act, slots, *merged, hidden, ow, place)
    return out.reshape(VZ, VX, VY, CH).transpose(1, 2, 0, 3)


def solution(mesh):
    placed = (
        P("gx", "gy", None, None),
        P("gx", "gy", None),
        P("gx", "gy", None, None),
        P("gx", "gy", None, None),
        P("gx", None, None),
        P(),
        P(),
        P(),
        P(),
        P(),
        P(),
    )
    return jax.shard_map(
        per_device, mesh=mesh, in_specs=placed, out_specs=P("gx", "gy", None, None), check_vma=False
    )
```

```python
import math

import jax
import jax.numpy as jnp
from jax import lax
from jax.experimental import pallas as pl
from jax.experimental.pallas import tpu as pltpu
from jax.sharding import PartitionSpec as P

CH = 256
HEADS = 8
HEAD_DIM = 32
EDGE = 4
VX, VY, VZ = 8, 8, 4
ROWS = VX * VY * VZ
WINDOWS = 4
ACT_MAX = 3
PARENTS = 4
TOK = 128
LANES = 128
PACK = 144
SLOTS = 4
CHIP = 2 * SLOTS
RING, LINE, CORES = 8, 4, 2
PAIRS = LINE * ACT_MAX * PARENTS
SCALE = math.log2(math.e) / math.sqrt(HEAD_DIM)
LOWEST = -3e38
F32 = jnp.float32
BF16 = jnp.bfloat16
VMEM = pl.BlockSpec(memory_space=pltpu.VMEM)
SMEM = pl.BlockSpec(memory_space=pltpu.SMEM)
ANY = pl.BlockSpec(memory_space=pl.ANY)
HBM = pl.BlockSpec(memory_space=pltpu.HBM)
NT = (((1,), (1,)), ((), ()))


def row_mask(act_ref):
    low = lax.broadcasted_iota(jnp.int32, (VY, CH), 0) < EDGE
    flags = [act_ref[w].astype(F32) for w in range(WINDOWS)]
    halves = [jnp.where(low, flags[2 * b], flags[2 * b + 1]) for b in range(2)]
    return jnp.concatenate(
        [jnp.broadcast_to(half[None], (EDGE, VY, CH)) for half in halves], axis=0
    )


def rank(act_ref, w):
    place = jnp.int32(0)
    for before in range(w):
        place = place + act_ref[before]
    return place


def placement():
    row = lax.broadcasted_iota(jnp.int32, (ROWS, LANES), 0)
    lane = lax.broadcasted_iota(jnp.int32, (ROWS, LANES), 1)
    query = (row >> 6) * 16 + ((row >> 3) & 3) * 4 + (row & 3)
    return query == (lane & 63), ((row >> 5) & 1) * 2 + ((row >> 2) & 1), lane


def face_kernel(act_ref, owner_ref, slot_ref, latent_ref, gain_ref, xa_ref, xb_ref, ya_ref, yb_ref, extra_ref):
    mask = row_mask(act_ref)
    gain = gain_ref[...].reshape(1, 1, CH)

    def normed(values, flags):
        scale = lax.rsqrt(jnp.mean(values * values, axis=-1, keepdims=True) + 1e-06)
        return (flags * values * scale * gain).astype(BF16)

    for side, ref in ((0, xa_ref), (VX - 1, xb_ref)):
        ref[...] = normed(latent_ref[:, side], mask[side][None])
    for side, ref in ((0, ya_ref), (VY - 1, yb_ref)):
        ref[...] = normed(latent_ref[:, :, side, :], mask[:, side, :][None])
    row = lax.broadcasted_iota(jnp.int32, (16, LANES), 0)
    lane = lax.broadcasted_iota(jnp.int32, (16, LANES), 1)
    for s in range(ACT_MAX):
        extra = jnp.full((16, LANES), -1.0, F32)
        for w in range(WINDOWS):
            here = (act_ref[w] > 0) & (rank(act_ref, w) == s)
            for p in range(PARENTS):
                code = owner_ref[w * PARENTS + p] * SLOTS + slot_ref[w * PARENTS + p]
                code = jnp.where(here, code, -1).astype(F32)
                extra = jnp.where((row == 0) & (lane == p), jnp.maximum(extra, code), extra)
        extra_ref[s] = extra.astype(BF16)


def conv_kernel(
    act_ref, latent_ref, xlo_ref, xhi_ref, ylo_ref, yhi_ref, ngain_ref, bias_ref,
    again_ref, weight_ref, qw_ref, extra_ref, hidden_ref, query_ref,
    frame, weights, sems,
):
    copies = [
        pltpu.make_async_copy(weight_ref.at[pl.ds(3 * ab, 3)], weights.at[pl.ds(3 * ab, 3)], sems.at[ab])
        for ab in range(9)
    ]
    for copy in copies:
        copy.start()
    latent = latent_ref[...]
    mask = row_mask(act_ref)[None]
    scale = lax.rsqrt(jnp.mean(latent * latent, axis=-1, keepdims=True) + 1e-06)
    normed = mask * latent * scale * ngain_ref[...].reshape(1, 1, 1, CH)
    frame[1, :, 1 : VX + 1] = normed
    frame[1, :, 0] = xlo_ref[...].astype(F32)
    frame[1, :, VX + 1] = xhi_ref[...].astype(F32)
    ylo = ylo_ref[...].astype(F32)
    yhi = yhi_ref[...].astype(F32)
    first = lax.broadcasted_iota(jnp.int32, (VY, CH), 0) == 0
    last = lax.broadcasted_iota(jnp.int32, (VY, CH), 0) == VY - 1
    for z in range(VZ):
        for x in range(VX + 2):
            r = z * (VX + 2) + x
            here = frame[1, z, x]
            frame[0, z, x] = jnp.where(first, ylo[r : r + 1, :], pltpu.roll(here, 1, 0))
            frame[2, z, x] = jnp.where(last, yhi[r : r + 1, :], pltpu.roll(here, VY - 1, 0))
    mid = jnp.zeros((ROWS, CH), F32)
    up = jnp.zeros((ROWS - 64, CH), F32)
    down = jnp.zeros((ROWS - 64, CH), F32)
    for ab in range(9):
        copies[ab].wait()
        a, b = ab // 3, ab % 3
        slab = frame[b, :, a : a + VX].reshape(ROWS, CH).astype(BF16)
        up = up + jnp.dot(slab[: ROWS - 64], weights[3 * ab], preferred_element_type=F32)
        mid = mid + jnp.dot(slab, weights[3 * ab + 1], preferred_element_type=F32)
        down = down + jnp.dot(slab[64:], weights[3 * ab + 2], preferred_element_type=F32)
    gap = jnp.zeros((64, CH), F32)
    conv = mid + jnp.concatenate([gap, up], 0) + jnp.concatenate([down, gap], 0) + bias_ref[...]
    flat_mask = jnp.broadcast_to(mask, (VZ, VX, VY, CH)).reshape(ROWS, CH)
    hidden = latent.reshape(ROWS, CH) + flat_mask * (conv / (1.0 + jnp.exp(-conv)))
    hidden_ref[...] = hidden
    scale = lax.rsqrt(jnp.mean(hidden * hidden, axis=-1, keepdims=True) + 1e-06)
    query_in = (hidden * scale * again_ref[...]).astype(BF16)
    queries = jnp.dot(query_in, qw_ref[...], preferred_element_type=F32).T.astype(BF16)
    left = lax.broadcasted_iota(jnp.int32, (HEAD_DIM, LANES), 1) < 64
    query_ref[:, :LANES, :] = jnp.zeros((ACT_MAX, LANES, LANES), BF16)
    query_ref[:, LANES:, :] = extra_ref[...]
    fits, window, _ = placement()
    for w in range(WINDOWS):
        @pl.when(act_ref[w] > 0)
        def _(w=w):
            place = jnp.where(fits & (window == w), 1.0, 0.0).astype(BF16)
            both = jnp.dot(queries, place, preferred_element_type=F32)
            packed = [
                jnp.where(left, both[64 * j : 64 * j + 32], both[64 * j + 32 : 64 * j + 64]) for j in range(4)
            ]
            query_ref[rank(act_ref, w), :LANES, :] = jnp.concatenate(packed, axis=0).astype(BF16)


def attend_kernel(here_ref, *refs):
    query_refs, kv_refs, out_refs = refs[:LINE], refs[LINE : LINE + RING], refs[LINE + RING : 2 * LINE + RING]
    codes, code_ref, held, blocks, sums, peak, total, sems, code_sem = refs[2 * LINE + RING :]
    ring, line, core = here_ref[0], here_ref[1], here_ref[2]
    for source in range(LINE):
        for s in range(ACT_MAX):
            codes[source * ACT_MAX + s] = query_refs[source][s, LANES:, :].astype(F32).astype(jnp.int32)
    listing = pltpu.make_async_copy(codes, code_ref, code_sem)
    listing.start()
    blocks[...] = jnp.zeros_like(blocks)
    listing.wait()

    def owned(n):
        code = code_ref[n // PARENTS, 0, n % PARENTS]
        owner = code >> 2
        return (code >= 0) & (((owner >> 1) & 3) == line), ((owner >> 3) - ring) & 7, owner & 1, code & 3

    def arrival(n):
        return pltpu.make_async_copy(kv_refs[0].at[0], held.at[n], sems.at[n])

    def begin(n, carry):
        mine, ahead, owner_core, slot = owned(n)
        steps = jnp.where((ahead > 4) | ((ahead == 4) & (core == 0)), RING - ahead, ahead)
        bearer = jnp.where(ahead == 0, core, jnp.where((ahead > 4) | ((ahead == 4) & (core == 0)), 0, 1))
        array = jnp.where((ahead == 0) | (bearer == core), steps, 4 + steps)
        index = jnp.where(owner_core == bearer, 0, SLOTS) + slot
        for k in range(RING):
            @pl.when(mine & (array == k))
            def _(k=k):
                pltpu.make_async_copy(kv_refs[k].at[index], held.at[n], sems.at[n]).start()
        return carry

    lax.fori_loop(0, PAIRS, begin, 0)
    left = lax.broadcasted_iota(jnp.int32, (HEAD_DIM, LANES), 1) < 64
    for source in range(LINE):
        query_ref, out_ref = query_refs[source], out_refs[source]

        def window(s, carry, source=source, query_ref=query_ref, out_ref=out_ref):
            base = (source * ACT_MAX + s) * PARENTS
            found = owned(base)[0]
            for p in range(1, PARENTS):
                found = found | owned(base + p)[0]

            @pl.when(jnp.logical_not(found))
            def _():
                out_ref[s, :LANES, :] = jnp.zeros((LANES, LANES), BF16)
                rows = lax.broadcasted_iota(jnp.int32, (PACK - LANES, LANES), 0)
                out_ref[s, LANES:, :] = jnp.where(rows < 4, LOWEST, 0.0).astype(BF16)

            @pl.when(found)
            def _():
                for j in range(4):
                    pair = query_ref[s, 32 * j : 32 * j + 32, :].astype(F32)
                    lanes = slice(LANES * j, LANES * j + LANES)
                    blocks[64 * j : 64 * j + 32, lanes] = jnp.where(left, pair, 0.0).astype(BF16)
                    blocks[64 * j + 32 : 64 * j + 64, lanes] = jnp.where(left, 0.0, pair).astype(BF16)
                sums[...] = jnp.zeros_like(sums)
                peak[...] = jnp.full_like(peak, LOWEST)
                total[...] = jnp.zeros_like(total)

                def parent(p, carry):
                    n = base + p

                    @pl.when(owned(n)[0])
                    def _():
                        arrival(n).wait()
                        for g in range(2):
                            half = slice(LANES * g, LANES * g + LANES)
                            wide = slice(256 * g, 256 * g + 256)
                            scores = jnp.dot(held[n, :, half], blocks[half, wide], preferred_element_type=F32)
                            old = peak[:, wide]
                            new = jnp.maximum(old, jnp.max(scores, axis=0, keepdims=True))
                            lifted = jnp.exp2((scores - new) * SCALE)
                            fade = jnp.exp2((old - new) * SCALE)
                            peak[:, wide] = new
                            total[:, wide] = total[:, wide] * fade + jnp.sum(lifted, axis=0, keepdims=True)
                            mixed = jnp.dot(
                                held[n, :, CH + LANES * g : CH + LANES * g + LANES].T,
                                lifted.astype(BF16), preferred_element_type=F32,
                            )
                            for jj in range(2):
                                rows = slice(64 * (2 * g + jj), 64 * (2 * g + jj) + 64)
                                cut = slice(LANES * jj, LANES * jj + LANES)
                                sums[rows, :] = sums[rows, :] * fade[:, cut] + mixed[64 * jj : 64 * jj + 64, cut]
                    return carry

                lax.fori_loop(0, PARENTS, parent, 0)
                levels = []
                for j in range(4):
                    lanes = slice(LANES * j, LANES * j + LANES)
                    kept = jnp.where(left, sums[64 * j : 64 * j + 32, :], sums[64 * j + 32 : 64 * j + 64, :])
                    out_ref[s, 32 * j : 32 * j + 32, :] = (kept / total[:, lanes]).astype(BF16)
                    levels.append(peak[:, lanes] * SCALE + jnp.log2(total[:, lanes]))
                level = jnp.concatenate(levels, axis=0)
                high = level.astype(BF16).astype(F32)
                middle = (level - high).astype(BF16).astype(F32)
                low = level - high - middle
                stats = jnp.concatenate([high, middle, low, jnp.zeros_like(low)], axis=0)
                out_ref[s, LANES:, :] = stats.astype(BF16)
            return carry

        lax.fori_loop(0, ACT_MAX, window, 0)


def merge_kernel(act_ref, *refs):
    part_refs = refs[:LINE]
    hidden_ref, ow_ref, out_ref, mixed, attended = refs[LINE:]
    for s in range(ACT_MAX):
        stats = [ref[s, LANES:, :].astype(F32) for ref in part_refs]
        levels = [one[0:4] + one[4:8] + one[8:12] for one in stats]
        top = jnp.maximum(jnp.maximum(levels[0], levels[1]), jnp.maximum(levels[2], levels[3]))
        shares = [jnp.exp2(level - top) for level in levels]
        whole = shares[0] + shares[1] + shares[2] + shares[3]
        for j in range(4):
            rows = slice(32 * j, 32 * j + 32)
            value = jnp.zeros((HEAD_DIM, LANES), F32)
            for ref, share in zip(part_refs, shares):
                value = value + ref[s, rows, :].astype(F32) * (share / whole)[j : j + 1, :]
            mixed[s, rows, :] = value.astype(BF16)
    attended[...] = jnp.zeros_like(attended)
    fits, window, lane = placement()
    for w in range(WINDOWS):
        @pl.when(act_ref[w] > 0)
        def _(w=w):
            block = mixed[rank(act_ref, w)]
            for side in range(2):
                place = jnp.where(fits & (window == w) & ((lane >> 6) == side), 1.0, 0.0).astype(BF16)
                attended[side] += lax.dot_general(place, block, NT, preferred_element_type=F32)
    projected = jnp.zeros((ROWS, CH), F32)
    for side in range(2):
        weight = jnp.concatenate([ow_ref[64 * j + 32 * side : 64 * j + 32 * side + 32, :] for j in range(4)], axis=0)
        projected = projected + jnp.dot(attended[side].astype(BF16), weight, preferred_element_type=F32)
    mask = jnp.broadcast_to(row_mask(act_ref)[None], (VZ, VX, VY, CH)).reshape(ROWS, CH)
    out_ref[...] = mask * (hidden_ref[...] + projected)


def shift(block, axis, step):
    count = lax.axis_size(axis)
    return lax.ppermute(block, axis, [(i, i + step) for i in range(count) if 0 <= i + step < count])


def after(block, *others):
    return lax.optimization_barrier((block, *others))[0]


def move(block, rule):
    pairs = []
    for i in range(RING * LINE * CORES):
        ring, line, core = rule(i // (LINE * CORES), i // CORES % LINE, i % CORES)
        pairs.append((i, (ring % RING * LINE + line % LINE) * CORES + core))
    return lax.ppermute(block, "gx", pairs)


def per_device(
    latent, active, parent_owner, parent_slot, coarse_kv, norm_gain, conv_weight, conv_bias,
    attn_gain, q_weight, out_weight,
):
    def swapped(block):
        return move(block, lambda ring, line, core: (ring, line, 1 - core))

    def ringed(block):
        return move(block, lambda ring, line, core: (ring + 1 - 2 * core, line, core))

    chip = jnp.concatenate([coarse_kv, swapped(coarse_kv)], axis=0)
    first = ringed(chip)

    act = active.reshape(WINDOWS)
    turned = latent.transpose(2, 0, 1, 3)
    face = jax.ShapeDtypeStruct((VZ, VX, CH), BF16)
    x_first, x_last, y_first, y_last, extra = pl.pallas_call(
        face_kernel,
        out_shape=[face] * 4 + [jax.ShapeDtypeStruct((ACT_MAX, PACK - LANES, LANES), BF16)],
        in_specs=[SMEM] * 3 + [VMEM] * 2,
        out_specs=[VMEM] * 5,
        name="faces",
    )(act, parent_owner.reshape(-1), parent_slot.reshape(-1), turned, norm_gain.reshape(1, CH))
    x_last = after(x_last, chip)
    x_low, x_high = shift(x_last, "gx", 1), shift(x_first, "gx", -1)
    y_first = jnp.concatenate([x_low[:, :1], y_first, x_high[:, :1]], axis=1).reshape(-1, CH)
    y_last = jnp.concatenate([x_low[:, -1:], y_last, x_high[:, -1:]], axis=1).reshape(-1, CH)
    y_low, y_high = shift(y_last, "gy", 1), shift(y_first, "gy", -1)

    second = ringed(after(first, y_low, y_high))
    hidden, query = pl.pallas_call(
        conv_kernel,
        out_shape=(
            jax.ShapeDtypeStruct((ROWS, CH), F32),
            jax.ShapeDtypeStruct((ACT_MAX, PACK, LANES), BF16),
        ),
        in_specs=[SMEM] + [VMEM] * 8 + [HBM] + [VMEM] * 2,
        out_specs=(VMEM, VMEM),
        scratch_shapes=[
            pltpu.VMEM((3, VZ, VX + 2, VY, CH), F32),
            pltpu.VMEM((27, CH, CH), BF16),
            pltpu.SemaphoreType.DMA((9,)),
        ],
        compiler_params=pltpu.CompilerParams(vmem_limit_bytes=20 << 20),
        cost_estimate=pl.CostEstimate(flops=2 * 27 * ROWS * CH * CH, bytes_accessed=5 << 20, transcendentals=ROWS * CH),
        name="conv",
    )(
        act, turned, x_low, x_high, y_low, y_high, norm_gain.reshape(1, CH),
        conv_bias.reshape(1, CH), attn_gain.reshape(1, CH), conv_weight, q_weight, extra,
    )

    def along(block, step):
        return move(block, lambda ring, line, core: (ring, line + step, core))

    index = lax.axis_index("gx")
    here = jnp.stack([index // (LINE * CORES), index // CORES % LINE, index % CORES]).astype(jnp.int32)
    queries = [query] + [along(query, d) for d in range(1, LINE)]
    third = ringed(after(second, *queries))
    fourth = ringed(third)
    kv_all = [chip, first, second, third, fourth]
    kv_all = kv_all + [swapped(after(first, *queries)), swapped(after(second, *queries)), swapped(third)]
    parts = pl.pallas_call(
        attend_kernel,
        out_shape=[jax.ShapeDtypeStruct((ACT_MAX, PACK, LANES), BF16)] * LINE,
        in_specs=[SMEM] + [VMEM] * LINE + [ANY] * RING,
        out_specs=[VMEM] * LINE,
        scratch_shapes=[
            pltpu.VMEM((LINE * ACT_MAX, PACK - LANES, LANES), jnp.int32),
            pltpu.SMEM((LINE * ACT_MAX, PACK - LANES, LANES), jnp.int32),
            pltpu.VMEM((PAIRS, TOK, 2 * CH), BF16),
            pltpu.VMEM((CH, 2 * CH), BF16),
            pltpu.VMEM((CH, LANES), F32),
            pltpu.VMEM((1, 2 * CH), F32),
            pltpu.VMEM((1, 2 * CH), F32),
            pltpu.SemaphoreType.DMA((PAIRS,)),
            pltpu.SemaphoreType.DMA,
        ],
        compiler_params=pltpu.CompilerParams(vmem_limit_bytes=16 << 20),
        name="attend",
    )(here, *queries, *kv_all)

    merged = [parts[0]] + [along(parts[d], -d) for d in range(1, LINE)]
    out = pl.pallas_call(
        merge_kernel,
        out_shape=jax.ShapeDtypeStruct((ROWS, CH), F32),
        in_specs=[SMEM] + [VMEM] * (LINE + 2),
        out_specs=VMEM,
        scratch_shapes=[
            pltpu.VMEM((ACT_MAX, LANES, LANES), BF16),
            pltpu.VMEM((2, ROWS, LANES), F32),
        ],
        compiler_params=pltpu.CompilerParams(vmem_limit_bytes=16 << 20),
        name="merge",
    )(act, *merged, hidden, out_weight)
    return out.reshape(VZ, VX, VY, CH).transpose(1, 2, 0, 3)


def solution(mesh):
    placed = (
        P("gx", "gy", None, None),
        P("gx", "gy", None),
        P("gx", "gy", None, None),
        P("gx", "gy", None, None),
        P("gx", None, None),
        P(),
        P(),
        P(),
        P(),
        P(),
        P(),
    )
    return jax.shard_map(
        per_device, mesh=mesh, in_specs=placed, out_specs=P("gx", "gy", None, None), check_vma=False
    )
```

```python
import math

import jax
import jax.numpy as jnp
from jax import lax
from jax.experimental import pallas as pl
from jax.experimental.pallas import tpu as pltpu
from jax.sharding import PartitionSpec as P

CH = 256
HEADS = 8
HEAD_DIM = 32
EDGE = 4
VX, VY, VZ = 8, 8, 4
ROWS = VX * VY * VZ
WINDOWS = 4
ACT_MAX = 3
PARENTS = 4
TOK = 128
LANES = 128
PACK = 144
SLOTS = 4
CHIP = 2 * SLOTS
RING, LINE, CORES = 8, 4, 2
PAIRS = LINE * ACT_MAX * PARENTS
GROUP = 4
SCALE = math.log2(math.e) / math.sqrt(HEAD_DIM)
LOWEST = -3e38
F32 = jnp.float32
BF16 = jnp.bfloat16
VMEM = pl.BlockSpec(memory_space=pltpu.VMEM)
SMEM = pl.BlockSpec(memory_space=pltpu.SMEM)
ANY = pl.BlockSpec(memory_space=pl.ANY)
HBM = pl.BlockSpec(memory_space=pltpu.HBM)
NT = (((1,), (1,)), ((), ()))


def row_mask(act_ref):
    low = lax.broadcasted_iota(jnp.int32, (VY, CH), 0) < EDGE
    flags = [act_ref[w // 2, w % 2, 0].astype(F32) for w in range(WINDOWS)]
    halves = [jnp.where(low, flags[2 * b], flags[2 * b + 1]) for b in range(2)]
    return jnp.concatenate(
        [jnp.broadcast_to(half[None], (EDGE, VY, CH)) for half in halves], axis=0
    )


def rank(act_ref, w):
    place = jnp.int32(0)
    for before in range(w):
        place = place + act_ref[before // 2, before % 2, 0]
    return place


def placement():
    row = lax.broadcasted_iota(jnp.int32, (ROWS, LANES), 0)
    lane = lax.broadcasted_iota(jnp.int32, (ROWS, LANES), 1)
    query = (row >> 6) * 16 + ((row >> 3) & 3) * 4 + (row & 3)
    return query == (lane & 63), ((row >> 5) & 1) * 2 + ((row >> 2) & 1), lane


def face_kernel(
    act_ref, owner_ref, slot_ref, latent_ref, gain_ref, xa_ref, xb_ref, ya_ref, yb_ref, extra_ref, turned_ref
):
    for z in range(VZ):
        for x in range(VX):
            turned_ref[z, x] = latent_ref[x, :, z, :]
    mask = row_mask(act_ref)
    gain = gain_ref[...].reshape(1, 1, CH)

    def normed(values, flags):
        scale = lax.rsqrt(jnp.mean(values * values, axis=-1, keepdims=True) + 1e-06)
        return (flags * values * scale * gain).astype(BF16)

    for side, ref in ((0, xa_ref), (VX - 1, xb_ref)):
        ref[...] = normed(turned_ref[:, side], mask[side][None])
    for side, ref in ((0, ya_ref), (VY - 1, yb_ref)):
        ref[...] = normed(turned_ref[:, :, side, :], mask[:, side, :][None])
    row = lax.broadcasted_iota(jnp.int32, (16, LANES), 0)
    lane = lax.broadcasted_iota(jnp.int32, (16, LANES), 1)
    for s in range(ACT_MAX):
        extra = jnp.full((16, LANES), -1.0, F32)
        for w in range(WINDOWS):
            here = (act_ref[w // 2, w % 2, 0] > 0) & (rank(act_ref, w) == s)
            for p in range(PARENTS):
                code = owner_ref[0, 0, w, p] * SLOTS + slot_ref[0, 0, w, p]
                code = jnp.where(here, code, -1).astype(F32)
                extra = jnp.where((row == 0) & (lane == p), jnp.maximum(extra, code), extra)
        extra_ref[s] = extra.astype(BF16)


def conv_kernel(
    act_ref, latent_ref, xlo_ref, xhi_ref, ylo_ref, yhi_ref, ngain_ref, bias_ref,
    again_ref, weight_ref, qw_ref, extra_ref, hidden_ref, query_ref,
    frame, weights, sems,
):
    copies = [
        pltpu.make_async_copy(weight_ref.at[pl.ds(3 * ab, 3)], weights.at[pl.ds(3 * ab, 3)], sems.at[ab])
        for ab in range(9)
    ]
    for copy in copies:
        copy.start()
    latent = latent_ref[...]
    mask = row_mask(act_ref)[None]
    scale = lax.rsqrt(jnp.mean(latent * latent, axis=-1, keepdims=True) + 1e-06)
    normed = mask * latent * scale * ngain_ref[...].reshape(1, 1, 1, CH)
    frame[1, :, 1 : VX + 1] = normed
    frame[1, :, 0] = xlo_ref[...].astype(F32)
    frame[1, :, VX + 1] = xhi_ref[...].astype(F32)
    ylo = ylo_ref[...].astype(F32)
    yhi = yhi_ref[...].astype(F32)
    first = lax.broadcasted_iota(jnp.int32, (VY, CH), 0) == 0
    last = lax.broadcasted_iota(jnp.int32, (VY, CH), 0) == VY - 1
    for z in range(VZ):
        for x in range(VX + 2):
            r = z * (VX + 2) + x
            here = frame[1, z, x]
            frame[0, z, x] = jnp.where(first, ylo[r : r + 1, :], pltpu.roll(here, 1, 0))
            frame[2, z, x] = jnp.where(last, yhi[r : r + 1, :], pltpu.roll(here, VY - 1, 0))
    mid = jnp.zeros((ROWS, CH), F32)
    up = jnp.zeros((ROWS - 64, CH), F32)
    down = jnp.zeros((ROWS - 64, CH), F32)
    for ab in range(9):
        copies[ab].wait()
        a, b = ab // 3, ab % 3
        slab = frame[b, :, a : a + VX].reshape(ROWS, CH).astype(BF16)
        up = up + jnp.dot(slab[: ROWS - 64], weights[3 * ab], preferred_element_type=F32)
        mid = mid + jnp.dot(slab, weights[3 * ab + 1], preferred_element_type=F32)
        down = down + jnp.dot(slab[64:], weights[3 * ab + 2], preferred_element_type=F32)
    gap = jnp.zeros((64, CH), F32)
    conv = mid + jnp.concatenate([gap, up], 0) + jnp.concatenate([down, gap], 0) + bias_ref[...]
    flat_mask = jnp.broadcast_to(mask, (VZ, VX, VY, CH)).reshape(ROWS, CH)
    hidden = latent.reshape(ROWS, CH) + flat_mask * (conv / (1.0 + jnp.exp(-conv)))
    hidden_ref[...] = hidden
    scale = lax.rsqrt(jnp.mean(hidden * hidden, axis=-1, keepdims=True) + 1e-06)
    query_in = (hidden * scale * again_ref[...]).astype(BF16)
    queries = jnp.dot(query_in, qw_ref[...], preferred_element_type=F32).T.astype(BF16)
    left = lax.broadcasted_iota(jnp.int32, (HEAD_DIM, LANES), 1) < 64
    query_ref[:, :LANES, :] = jnp.zeros((ACT_MAX, LANES, LANES), BF16)
    query_ref[:, LANES:, :] = extra_ref[...]
    fits, window, _ = placement()
    for w in range(WINDOWS):
        @pl.when(act_ref[w // 2, w % 2, 0] > 0)
        def _(w=w):
            place = jnp.where(fits & (window == w), 1.0, 0.0).astype(BF16)
            both = jnp.dot(queries, place, preferred_element_type=F32)
            packed = [
                jnp.where(left, both[64 * j : 64 * j + 32], both[64 * j + 32 : 64 * j + 64]) for j in range(4)
            ]
            query_ref[rank(act_ref, w), :LANES, :] = jnp.concatenate(packed, axis=0).astype(BF16)


def attend_kernel(here_ref, *refs):
    query_refs, kv_refs, out_refs = refs[:LINE], refs[LINE : LINE + RING], refs[LINE + RING : 2 * LINE + RING]
    codes, code_ref, list_ref, held, blocks, values, levels, sems, code_sem = refs[2 * LINE + RING :]
    here = here_ref[0]
    ring, line, core = here >> 3, (here >> 1) & 3, here & 1
    for source in range(LINE):
        for s in range(ACT_MAX):
            codes[source * ACT_MAX + s] = query_refs[source][s, LANES:, :].astype(F32).astype(jnp.int32)
    listing = pltpu.make_async_copy(codes, code_ref, code_sem)
    listing.start()
    left = lax.broadcasted_iota(jnp.int32, (HEAD_DIM, LANES), 1) < 64
    none = jnp.zeros((64, LANES), BF16)
    for source in range(LINE):
        for s in range(ACT_MAX):
            w = source * ACT_MAX + s
            for j in range(4):
                pair = query_refs[source][s, 32 * j : 32 * j + 32, :].astype(F32)
                lanes = slice(LANES * (j % 2), LANES * (j % 2) + LANES)
                beside = slice(LANES * (1 - j % 2), LANES * (1 - j % 2) + LANES)
                blocks[w, 64 * j : 64 * j + 32, lanes] = jnp.where(left, pair, 0.0).astype(BF16)
                blocks[w, 64 * j + 32 : 64 * j + 64, lanes] = jnp.where(left, 0.0, pair).astype(BF16)
                blocks[w, 64 * j : 64 * j + 64, beside] = none
    listing.wait()

    def owned(n):
        code = code_ref[n // PARENTS, 0, n % PARENTS]
        owner = code >> 2
        return (code >= 0) & (((owner >> 1) & 3) == line), ((owner >> 3) - ring) & 7, owner & 1, code & 3

    def begin(n, count):
        mine, ahead, owner_core, slot = owned(n)
        below = (ahead > 4) | ((ahead == 4) & (core == 0))
        steps = jnp.where(below, RING - ahead, ahead)
        bearer = jnp.where(ahead == 0, core, jnp.where(below, 0, 1))
        array = jnp.where((ahead == 0) | (bearer == core), steps, 4 + steps)
        index = jnp.where(owner_core == bearer, 0, SLOTS) + slot

        @pl.when(mine)
        def _():
            list_ref[count] = n
            for k in range(RING):
                @pl.when(array == k)
                def _(k=k):
                    pltpu.make_async_copy(kv_refs[k].at[index], held.at[count], sems.at[count]).start()
        return count + mine.astype(jnp.int32)

    count = lax.fori_loop(0, PAIRS, begin, jnp.int32(0))

    def attend(at, w):
        for g in range(2):
            half = slice(LANES * g, LANES * g + LANES)
            scores = jnp.dot(held[at, :, half], blocks[w, half, :], preferred_element_type=F32)
            peak = jnp.max(scores, axis=0, keepdims=True)
            lifted = jnp.exp2((scores - peak) * SCALE)
            total = jnp.sum(lifted, axis=0, keepdims=True)
            turned = held[at, :, CH + LANES * g : CH + LANES * g + LANES].T
            mixed = jnp.dot(turned, lifted.astype(BF16), preferred_element_type=F32)
            for jj in range(2):
                cut = slice(LANES * jj, LANES * jj + LANES)
                row = 64 * jj
                kept = jnp.where(left, mixed[row : row + 32, cut], mixed[row + 32 : row + 64, cut])
                j = 2 * g + jj
                values[at, 32 * j : 32 * j + 32, :] = kept
                levels[at, j : j + 1, :] = peak[:, cut] * SCALE
                levels[at, 4 + j : 5 + j, :] = total[:, cut]

    def group(i, carry):
        for u in range(GROUP):
            at = i * GROUP + u

            @pl.when(at < count)
            def _(at=at):
                pltpu.make_async_copy(kv_refs[0].at[0], held.at[at], sems.at[at]).wait()
        window = [list_ref[jnp.minimum(i * GROUP + u, count - 1)] // PARENTS for u in range(GROUP)]
        for u in range(GROUP):
            attend(i * GROUP + u, window[u])
        return carry

    lax.fori_loop(0, (count + GROUP - 1) // GROUP, group, 0)
    rows = lax.broadcasted_iota(jnp.int32, (PACK - LANES, LANES), 0)
    done = jnp.int32(0)
    for source in range(LINE):
        out_ref = out_refs[source]
        for s in range(ACT_MAX):
            w = source * ACT_MAX + s
            matches = jnp.int32(0)
            for p in range(PARENTS):
                matches = matches + owned(w * PARENTS + p)[0].astype(jnp.int32)

            @pl.when(matches == 0)
            def _(s=s, out_ref=out_ref):
                out_ref[s, :LANES, :] = jnp.zeros((LANES, LANES), BF16)
                out_ref[s, LANES:, :] = jnp.where(rows < 4, LOWEST, 0.0).astype(BF16)

            @pl.when(matches > 0)
            def _(s=s, out_ref=out_ref, done=done, matches=matches):
                def join(k, state):
                    peak, total, value = state
                    new = jnp.maximum(peak, levels[done + k, 0:4, :])
                    fade, gain = jnp.exp2(peak - new), jnp.exp2(levels[done + k, 0:4, :] - new)
                    total = total * fade + levels[done + k, 4:8, :] * gain
                    value = jnp.concatenate(
                        [
                            value[32 * j : 32 * j + 32] * fade[j : j + 1]
                            + values[done + k, 32 * j : 32 * j + 32, :] * gain[j : j + 1]
                            for j in range(4)
                        ],
                        axis=0,
                    )
                    return new, total, value

                first = (levels[done, 0:4, :], levels[done, 4:8, :], values[done])
                peak, total, value = lax.fori_loop(1, matches, join, first)
                for j in range(4):
                    cut = slice(32 * j, 32 * j + 32)
                    out_ref[s, cut, :] = (value[cut] / total[j : j + 1]).astype(BF16)
                level = peak + jnp.log2(total)
                high = level.astype(BF16).astype(F32)
                middle = (level - high).astype(BF16).astype(F32)
                low = level - high - middle
                stats = jnp.concatenate([high, middle, low, jnp.zeros_like(low)], axis=0)
                out_ref[s, LANES:, :] = stats.astype(BF16)

            done = done + matches


def merge_kernel(act_ref, *refs):
    part_refs = refs[:LINE]
    hidden_ref, ow_ref, out_ref, mixed, attended = refs[LINE:]
    for s in range(ACT_MAX):
        stats = [ref[s, LANES:, :].astype(F32) for ref in part_refs]
        levels = [one[0:4] + one[4:8] + one[8:12] for one in stats]
        top = jnp.maximum(jnp.maximum(levels[0], levels[1]), jnp.maximum(levels[2], levels[3]))
        shares = [jnp.exp2(level - top) for level in levels]
        whole = shares[0] + shares[1] + shares[2] + shares[3]
        for j in range(4):
            rows = slice(32 * j, 32 * j + 32)
            value = jnp.zeros((HEAD_DIM, LANES), F32)
            for ref, share in zip(part_refs, shares):
                value = value + ref[s, rows, :].astype(F32) * (share / whole)[j : j + 1, :]
            mixed[s, rows, :] = value.astype(BF16)
    attended[...] = jnp.zeros_like(attended)
    fits, window, lane = placement()
    for w in range(WINDOWS):
        @pl.when(act_ref[w // 2, w % 2, 0] > 0)
        def _(w=w):
            block = mixed[rank(act_ref, w)]
            for side in range(2):
                place = jnp.where(fits & (window == w) & ((lane >> 6) == side), 1.0, 0.0).astype(BF16)
                attended[side] += lax.dot_general(place, block, NT, preferred_element_type=F32)
    projected = jnp.zeros((ROWS, CH), F32)
    for side in range(2):
        weight = jnp.concatenate([ow_ref[64 * j + 32 * side : 64 * j + 32 * side + 32, :] for j in range(4)], axis=0)
        projected = projected + jnp.dot(attended[side].astype(BF16), weight, preferred_element_type=F32)
    mask = jnp.broadcast_to(row_mask(act_ref)[None], (VZ, VX, VY, CH)).reshape(ROWS, CH)
    out_ref[...] = mask * (hidden_ref[...] + projected)


def shift(block, axis, step):
    count = lax.axis_size(axis)
    return lax.ppermute(block, axis, [(i, i + step) for i in range(count) if 0 <= i + step < count])


def after(block, *others):
    return lax.optimization_barrier((block, *others))[0]


def move(block, rule):
    pairs = []
    for i in range(RING * LINE * CORES):
        ring, line, core = rule(i // (LINE * CORES), i // CORES % LINE, i % CORES)
        pairs.append((i, (ring % RING * LINE + line % LINE) * CORES + core))
    return lax.ppermute(block, "gx", pairs)


def per_device(
    latent, active, parent_owner, parent_slot, coarse_kv, norm_gain, conv_weight, conv_bias,
    attn_gain, q_weight, out_weight,
):
    def swapped(block):
        return move(block, lambda ring, line, core: (ring, line, 1 - core))

    def ringed(block):
        return move(block, lambda ring, line, core: (ring + 1 - 2 * core, line, core))

    chip = jnp.concatenate([coarse_kv, swapped(coarse_kv)], axis=0)
    first = ringed(chip)

    face = jax.ShapeDtypeStruct((VZ, VX, CH), BF16)
    x_first, x_last, y_first, y_last, extra, turned = pl.pallas_call(
        face_kernel,
        out_shape=[face] * 4 + [
            jax.ShapeDtypeStruct((ACT_MAX, PACK - LANES, LANES), BF16),
            jax.ShapeDtypeStruct((VZ, VX, VY, CH), F32),
        ],
        in_specs=[SMEM] * 3 + [VMEM] * 2,
        out_specs=[VMEM] * 6,
        compiler_params=pltpu.CompilerParams(vmem_limit_bytes=6 << 20),
        name="faces",
    )(active, parent_owner, parent_slot, latent, norm_gain.reshape(1, CH))
    x_last = after(x_last, chip)
    x_low, x_high = shift(x_last, "gx", 1), shift(x_first, "gx", -1)
    second = ringed(after(first, x_low, x_high))
    y_first, y_last = after(y_first, first), after(y_last, first)
    y_first = jnp.concatenate([x_low[:, :1], y_first, x_high[:, :1]], axis=1).reshape(-1, CH)
    y_last = jnp.concatenate([x_low[:, -1:], y_last, x_high[:, -1:]], axis=1).reshape(-1, CH)
    y_low, y_high = shift(y_last, "gy", 1), shift(y_first, "gy", -1)

    hidden, query = pl.pallas_call(
        conv_kernel,
        out_shape=(
            jax.ShapeDtypeStruct((ROWS, CH), F32),
            jax.ShapeDtypeStruct((ACT_MAX, PACK, LANES), BF16),
        ),
        in_specs=[SMEM] + [VMEM] * 8 + [HBM] + [VMEM] * 2,
        out_specs=(VMEM, VMEM),
        scratch_shapes=[
            pltpu.VMEM((3, VZ, VX + 2, VY, CH), F32),
            pltpu.VMEM((27, CH, CH), BF16),
            pltpu.SemaphoreType.DMA((9,)),
        ],
        compiler_params=pltpu.CompilerParams(vmem_limit_bytes=56 << 20),
        cost_estimate=pl.CostEstimate(flops=2 * 27 * ROWS * CH * CH, bytes_accessed=5 << 20, transcendentals=ROWS * CH),
        name="conv",
    )(
        active, turned, x_low, x_high, y_low, y_high, norm_gain.reshape(1, CH),
        conv_bias.reshape(1, CH), attn_gain.reshape(1, CH), conv_weight, q_weight, extra,
    )

    def along(block, step):
        return move(block, lambda ring, line, core: (ring, line + step, core))

    here = lax.axis_index("gx").astype(jnp.int32).reshape(1)
    third = ringed(after(second, query))
    query = after(query, second)
    queries = [query] + [along(query, d) for d in range(1, LINE)]
    fourth = ringed(after(third, *queries))
    kv_all = [chip, first, second, third, fourth]
    kv_all = kv_all + [swapped(after(first, *queries)), swapped(after(second, *queries)), swapped(third)]
    parts = pl.pallas_call(
        attend_kernel,
        out_shape=[jax.ShapeDtypeStruct((ACT_MAX, PACK, LANES), BF16)] * LINE,
        in_specs=[SMEM] + [VMEM] * LINE + [ANY] * RING,
        out_specs=[VMEM] * LINE,
        scratch_shapes=[
            pltpu.VMEM((LINE * ACT_MAX, PACK - LANES, LANES), jnp.int32),
            pltpu.SMEM((LINE * ACT_MAX, PACK - LANES, LANES), jnp.int32),
            pltpu.SMEM((PAIRS,), jnp.int32),
            pltpu.VMEM((PAIRS, TOK, 2 * CH), BF16),
            pltpu.VMEM((LINE * ACT_MAX, CH, CH), BF16),
            pltpu.VMEM((PAIRS, LANES, LANES), F32),
            pltpu.VMEM((PAIRS, 8, LANES), F32),
            pltpu.SemaphoreType.DMA((PAIRS,)),
            pltpu.SemaphoreType.DMA,
        ],
        compiler_params=pltpu.CompilerParams(vmem_limit_bytes=18 << 20),
        name="attend",
    )(here, *queries, *kv_all)

    merged = [parts[0]] + [along(parts[d], -d) for d in range(1, LINE)]
    out = pl.pallas_call(
        merge_kernel,
        out_shape=jax.ShapeDtypeStruct((ROWS, CH), F32),
        in_specs=[SMEM] + [VMEM] * (LINE + 2),
        out_specs=VMEM,
        scratch_shapes=[
            pltpu.VMEM((ACT_MAX, LANES, LANES), BF16),
            pltpu.VMEM((2, ROWS, LANES), F32),
        ],
        compiler_params=pltpu.CompilerParams(vmem_limit_bytes=8 << 20),
        name="merge",
    )(active, *merged, hidden, out_weight)
    return out.reshape(VZ, VX, VY, CH).transpose(1, 2, 0, 3)


def solution(mesh):
    placed = (
        P("gx", "gy", None, None),
        P("gx", "gy", None),
        P("gx", "gy", None, None),
        P("gx", "gy", None, None),
        P("gx", None, None),
        P(),
        P(),
        P(),
        P(),
        P(),
        P(),
    )
    return jax.shard_map(
        per_device, mesh=mesh, in_specs=placed, out_specs=P("gx", "gy", None, None), check_vma=False
    )
```

```python
import math

import jax
import jax.numpy as jnp
from jax import lax
from jax.experimental import pallas as pl
from jax.experimental.pallas import tpu as pltpu
from jax.sharding import PartitionSpec as P

CH = 256
HEADS = 8
HEAD_DIM = 32
EDGE = 4
VX, VY, VZ = 8, 8, 4
ROWS = VX * VY * VZ
WINDOWS = 4
ACT_MAX = 3
PARENTS = 4
TOK = 128
LANES = 128
PACK = 144
SLOTS = 4
CHIP = 2 * SLOTS
ARRAYS = 16
RING, LINE, CORES = 8, 4, 2
PAIRS = LINE * ACT_MAX * PARENTS
GROUP = 4
SCALE = math.log2(math.e) / math.sqrt(HEAD_DIM)
LOWEST = -3e38
F32 = jnp.float32
BF16 = jnp.bfloat16
VMEM = pl.BlockSpec(memory_space=pltpu.VMEM)
SMEM = pl.BlockSpec(memory_space=pltpu.SMEM)
ANY = pl.BlockSpec(memory_space=pl.ANY)
HBM = pl.BlockSpec(memory_space=pltpu.HBM)
NT = (((1,), (1,)), ((), ()))


def row_mask(act_ref):
    low = lax.broadcasted_iota(jnp.int32, (VY, CH), 0) < EDGE
    flags = [act_ref[w // 2, w % 2, 0].astype(F32) for w in range(WINDOWS)]
    halves = [jnp.where(low, flags[2 * b], flags[2 * b + 1]) for b in range(2)]
    return jnp.concatenate(
        [jnp.broadcast_to(half[None], (EDGE, VY, CH)) for half in halves], axis=0
    )


def rank(act_ref, w):
    place = jnp.int32(0)
    for before in range(w):
        place = place + act_ref[before // 2, before % 2, 0]
    return place


def placement():
    row = lax.broadcasted_iota(jnp.int32, (ROWS, LANES), 0)
    lane = lax.broadcasted_iota(jnp.int32, (ROWS, LANES), 1)
    query = (row >> 6) * 16 + ((row >> 3) & 3) * 4 + (row & 3)
    return query == (lane & 63), ((row >> 5) & 1) * 2 + ((row >> 2) & 1), lane


def face_kernel(
    act_ref, owner_ref, slot_ref, latent_ref, gain_ref, xa_ref, xb_ref, ya_ref, yb_ref, extra_ref, turned_ref
):
    for z in range(VZ):
        for x in range(VX):
            turned_ref[z, x] = latent_ref[x, :, z, :]
    mask = row_mask(act_ref)
    gain = gain_ref[...].reshape(1, 1, CH)

    def normed(values, flags):
        scale = lax.rsqrt(jnp.mean(values * values, axis=-1, keepdims=True) + 1e-06)
        return (flags * values * scale * gain).astype(BF16)

    for side, ref in ((0, xa_ref), (VX - 1, xb_ref)):
        ref[...] = normed(turned_ref[:, side], mask[side][None])
    for side, ref in ((0, ya_ref), (VY - 1, yb_ref)):
        ref[...] = normed(turned_ref[:, :, side, :], mask[:, side, :][None])
    row = lax.broadcasted_iota(jnp.int32, (16, LANES), 0)
    lane = lax.broadcasted_iota(jnp.int32, (16, LANES), 1)
    for s in range(ACT_MAX):
        extra = jnp.full((16, LANES), -1.0, F32)
        for w in range(WINDOWS):
            here = (act_ref[w // 2, w % 2, 0] > 0) & (rank(act_ref, w) == s)
            for p in range(PARENTS):
                code = owner_ref[0, 0, w, p] * SLOTS + slot_ref[0, 0, w, p]
                code = jnp.where(here, code, -1).astype(F32)
                extra = jnp.where((row == 0) & (lane == p), jnp.maximum(extra, code), extra)
        extra_ref[s] = extra.astype(BF16)


def conv_kernel(
    act_ref, latent_ref, xlo_ref, xhi_ref, ylo_ref, yhi_ref, ngain_ref, bias_ref,
    again_ref, weight_ref, qw_ref, extra_ref, hidden_ref, query_ref,
    frame, weights, sems,
):
    copies = [
        pltpu.make_async_copy(weight_ref.at[pl.ds(3 * ab, 3)], weights.at[pl.ds(3 * ab, 3)], sems.at[ab])
        for ab in range(9)
    ]
    for copy in copies:
        copy.start()
    latent = latent_ref[...]
    mask = row_mask(act_ref)[None]
    scale = lax.rsqrt(jnp.mean(latent * latent, axis=-1, keepdims=True) + 1e-06)
    normed = mask * latent * scale * ngain_ref[...].reshape(1, 1, 1, CH)
    frame[1, :, 1 : VX + 1] = normed
    frame[1, :, 0] = xlo_ref[...].astype(F32)
    frame[1, :, VX + 1] = xhi_ref[...].astype(F32)
    ylo = ylo_ref[...].astype(F32)
    yhi = yhi_ref[...].astype(F32)
    first = lax.broadcasted_iota(jnp.int32, (VY, CH), 0) == 0
    last = lax.broadcasted_iota(jnp.int32, (VY, CH), 0) == VY - 1
    for z in range(VZ):
        for x in range(VX + 2):
            r = z * (VX + 2) + x
            here = frame[1, z, x]
            frame[0, z, x] = jnp.where(first, ylo[r : r + 1, :], pltpu.roll(here, 1, 0))
            frame[2, z, x] = jnp.where(last, yhi[r : r + 1, :], pltpu.roll(here, VY - 1, 0))
    mid = jnp.zeros((ROWS, CH), F32)
    up = jnp.zeros((ROWS - 64, CH), F32)
    down = jnp.zeros((ROWS - 64, CH), F32)
    for ab in range(9):
        copies[ab].wait()
        a, b = ab // 3, ab % 3
        slab = frame[b, :, a : a + VX].reshape(ROWS, CH).astype(BF16)
        up = up + jnp.dot(slab[: ROWS - 64], weights[3 * ab], preferred_element_type=F32)
        mid = mid + jnp.dot(slab, weights[3 * ab + 1], preferred_element_type=F32)
        down = down + jnp.dot(slab[64:], weights[3 * ab + 2], preferred_element_type=F32)
    gap = jnp.zeros((64, CH), F32)
    conv = mid + jnp.concatenate([gap, up], 0) + jnp.concatenate([down, gap], 0) + bias_ref[...]
    flat_mask = jnp.broadcast_to(mask, (VZ, VX, VY, CH)).reshape(ROWS, CH)
    hidden = latent.reshape(ROWS, CH) + flat_mask * (conv / (1.0 + jnp.exp(-conv)))
    hidden_ref[...] = hidden
    scale = lax.rsqrt(jnp.mean(hidden * hidden, axis=-1, keepdims=True) + 1e-06)
    query_in = (hidden * scale * again_ref[...]).astype(BF16)
    queries = jnp.dot(query_in, qw_ref[...], preferred_element_type=F32).T.astype(BF16)
    left = lax.broadcasted_iota(jnp.int32, (HEAD_DIM, LANES), 1) < 64
    query_ref[:, :LANES, :] = jnp.zeros((ACT_MAX, LANES, LANES), BF16)
    query_ref[:, LANES:, :] = extra_ref[...]
    fits, window, _ = placement()
    for w in range(WINDOWS):
        @pl.when(act_ref[w // 2, w % 2, 0] > 0)
        def _(w=w):
            place = jnp.where(fits & (window == w), 1.0, 0.0).astype(BF16)
            both = jnp.dot(queries, place, preferred_element_type=F32)
            packed = [
                jnp.where(left, both[64 * j : 64 * j + 32], both[64 * j + 32 : 64 * j + 64]) for j in range(4)
            ]
            query_ref[rank(act_ref, w), :LANES, :] = jnp.concatenate(packed, axis=0).astype(BF16)


def attend_kernel(here_ref, *refs):
    query_refs, kv_refs, out_refs = refs[:LINE], refs[LINE : LINE + ARRAYS], refs[LINE + ARRAYS : 2 * LINE + ARRAYS]
    codes, code_ref, list_ref, match_ref, held, blocks, values, levels, sems, code_sem = refs[2 * LINE + ARRAYS :]
    here = here_ref[0]
    ring, line, core = here >> 3, (here >> 1) & 3, here & 1
    for source in range(LINE):
        for s in range(ACT_MAX):
            codes[source * ACT_MAX + s] = query_refs[source][s, LANES:, :].astype(F32).astype(jnp.int32)
    listing = pltpu.make_async_copy(codes, code_ref, code_sem)
    listing.start()
    left = lax.broadcasted_iota(jnp.int32, (HEAD_DIM, LANES), 1) < 64
    none = jnp.zeros((64, LANES), BF16)
    for source in range(LINE):
        for s in range(ACT_MAX):
            w = source * ACT_MAX + s
            for j in range(4):
                pair = query_refs[source][s, 32 * j : 32 * j + 32, :].astype(F32)
                lanes = slice(LANES * (j % 2), LANES * (j % 2) + LANES)
                beside = slice(LANES * (1 - j % 2), LANES * (1 - j % 2) + LANES)
                blocks[w, 64 * j : 64 * j + 32, lanes] = jnp.where(left, pair, 0.0).astype(BF16)
                blocks[w, 64 * j + 32 : 64 * j + 64, lanes] = jnp.where(left, 0.0, pair).astype(BF16)
                blocks[w, 64 * j : 64 * j + 64, beside] = none
    listing.wait()

    def fetch(w, count):
        def parents(count):
            for p in range(PARENTS):
                code = code_ref[w, 0, p]
                owner = code >> 2
                mine = ((owner >> 1) & 3) == line
                ahead, owner_core, slot = ((owner >> 3) - ring) & 7, owner & 1, code & 3
                below = ahead > 4
                steps = jnp.where(below, RING - ahead, ahead)
                brought = (ahead == 0) | (ahead == 4) | (below == (core == 0))
                own = owner_core == core
                array = jnp.where(
                    brought,
                    jnp.where(own, steps, jnp.where(ahead == 4, 12, 5 + steps)),
                    jnp.where(own, 12 + steps, 8 + steps),
                )

                @pl.when(mine)
                def _(count=count, array=array, slot=slot):
                    list_ref[count] = w
                    for quarter in range(0, ARRAYS, 4):
                        @pl.when((array >> 2) == quarter // 4)
                        def _(quarter=quarter):
                            for k in range(quarter, quarter + 4):
                                @pl.when(array == k)
                                def _(k=k):
                                    pltpu.make_async_copy(kv_refs[k].at[slot], held.at[count], sems.at[count]).start()
                count = count + mine.astype(jnp.int32)
            return count

        after = lax.cond(code_ref[w, 0, 0] >= 0, parents, lambda count: count, count)
        match_ref[w] = after - count
        return after

    count = lax.fori_loop(0, LINE * ACT_MAX, fetch, jnp.int32(0))

    def attend(at, w):
        for g in range(2):
            half = slice(LANES * g, LANES * g + LANES)
            scores = jnp.dot(held[at, :, half], blocks[w, half, :], preferred_element_type=F32)
            peak = jnp.max(scores, axis=0, keepdims=True)
            lifted = jnp.exp2((scores - peak) * SCALE)
            total = jnp.sum(lifted, axis=0, keepdims=True)
            turned = held[at, :, CH + LANES * g : CH + LANES * g + LANES].T
            mixed = jnp.dot(turned, lifted.astype(BF16), preferred_element_type=F32)
            for jj in range(2):
                cut = slice(LANES * jj, LANES * jj + LANES)
                row = 64 * jj
                kept = jnp.where(left, mixed[row : row + 32, cut], mixed[row + 32 : row + 64, cut])
                j = 2 * g + jj
                values[at, 32 * j : 32 * j + 32, :] = kept
                levels[at, j : j + 1, :] = peak[:, cut] * SCALE
                levels[at, 4 + j : 5 + j, :] = total[:, cut]

    def group(i, carry):
        for u in range(GROUP):
            at = i * GROUP + u

            @pl.when(at < count)
            def _(at=at):
                pltpu.make_async_copy(kv_refs[0].at[0], held.at[at], sems.at[at]).wait()
        window = [list_ref[jnp.minimum(i * GROUP + u, count - 1)] for u in range(GROUP)]
        for u in range(GROUP):
            attend(i * GROUP + u, window[u])
        return carry

    lax.fori_loop(0, (count + GROUP - 1) // GROUP, group, 0)
    rows = lax.broadcasted_iota(jnp.int32, (PACK - LANES, LANES), 0)
    done = jnp.int32(0)
    for source in range(LINE):
        out_ref = out_refs[source]
        for s in range(ACT_MAX):
            w = source * ACT_MAX + s
            matches = match_ref[w]

            @pl.when(matches == 0)
            def _(s=s, out_ref=out_ref):
                out_ref[s, :LANES, :] = jnp.zeros((LANES, LANES), BF16)
                out_ref[s, LANES:, :] = jnp.where(rows < 4, LOWEST, 0.0).astype(BF16)

            @pl.when(matches > 0)
            def _(s=s, out_ref=out_ref, done=done, matches=matches):
                def join(k, state):
                    peak, total, value = state
                    new = jnp.maximum(peak, levels[done + k, 0:4, :])
                    fade, gain = jnp.exp2(peak - new), jnp.exp2(levels[done + k, 0:4, :] - new)
                    total = total * fade + levels[done + k, 4:8, :] * gain
                    value = jnp.concatenate(
                        [
                            value[32 * j : 32 * j + 32] * fade[j : j + 1]
                            + values[done + k, 32 * j : 32 * j + 32, :] * gain[j : j + 1]
                            for j in range(4)
                        ],
                        axis=0,
                    )
                    return new, total, value

                first = (levels[done, 0:4, :], levels[done, 4:8, :], values[done])
                peak, total, value = lax.fori_loop(1, matches, join, first)
                for j in range(4):
                    cut = slice(32 * j, 32 * j + 32)
                    out_ref[s, cut, :] = (value[cut] / total[j : j + 1]).astype(BF16)
                level = peak + jnp.log2(total)
                high = level.astype(BF16).astype(F32)
                middle = (level - high).astype(BF16).astype(F32)
                low = level - high - middle
                stats = jnp.concatenate([high, middle, low, jnp.zeros_like(low)], axis=0)
                out_ref[s, LANES:, :] = stats.astype(BF16)

            done = done + matches


def merge_kernel(act_ref, *refs):
    part_refs = refs[:LINE]
    hidden_ref, ow_ref, out_ref, mixed, attended = refs[LINE:]
    for s in range(ACT_MAX):
        stats = [ref[s, LANES:, :].astype(F32) for ref in part_refs]
        levels = [one[0:4] + one[4:8] + one[8:12] for one in stats]
        top = jnp.maximum(jnp.maximum(levels[0], levels[1]), jnp.maximum(levels[2], levels[3]))
        shares = [jnp.exp2(level - top) for level in levels]
        whole = shares[0] + shares[1] + shares[2] + shares[3]
        for j in range(4):
            rows = slice(32 * j, 32 * j + 32)
            value = jnp.zeros((HEAD_DIM, LANES), F32)
            for ref, share in zip(part_refs, shares):
                value = value + ref[s, rows, :].astype(F32) * (share / whole)[j : j + 1, :]
            mixed[s, rows, :] = value.astype(BF16)
    attended[...] = jnp.zeros_like(attended)
    fits, window, lane = placement()
    for w in range(WINDOWS):
        @pl.when(act_ref[w // 2, w % 2, 0] > 0)
        def _(w=w):
            block = mixed[rank(act_ref, w)]
            for side in range(2):
                place = jnp.where(fits & (window == w) & ((lane >> 6) == side), 1.0, 0.0).astype(BF16)
                attended[side] += lax.dot_general(place, block, NT, preferred_element_type=F32)
    projected = jnp.zeros((ROWS, CH), F32)
    for side in range(2):
        weight = jnp.concatenate([ow_ref[64 * j + 32 * side : 64 * j + 32 * side + 32, :] for j in range(4)], axis=0)
        projected = projected + jnp.dot(attended[side].astype(BF16), weight, preferred_element_type=F32)
    mask = jnp.broadcast_to(row_mask(act_ref)[None], (VZ, VX, VY, CH)).reshape(ROWS, CH)
    out_ref[...] = mask * (hidden_ref[...] + projected)


def shift(block, axis, step):
    count = lax.axis_size(axis)
    return lax.ppermute(block, axis, [(i, i + step) for i in range(count) if 0 <= i + step < count])


def after(block, *others):
    return lax.optimization_barrier((block, *others))[0]


def move(block, rule):
    pairs = []
    for i in range(RING * LINE * CORES):
        ring, line, core = rule(i // (LINE * CORES), i // CORES % LINE, i % CORES)
        pairs.append((i, (ring % RING * LINE + line % LINE) * CORES + core))
    return lax.ppermute(block, "gx", pairs)


def per_device(
    latent, active, parent_owner, parent_slot, coarse_kv, norm_gain, conv_weight, conv_bias,
    attn_gain, q_weight, out_weight,
):
    def swapped(block):
        return move(block, lambda ring, line, core: (ring, line, 1 - core))

    def ringed(block):
        return move(block, lambda ring, line, core: (ring + 1 - 2 * core, line, core))

    a0, a1, b0 = coarse_kv, ringed(coarse_kv), swapped(coarse_kv)
    b1 = ringed(b0)

    face = jax.ShapeDtypeStruct((VZ, VX, CH), BF16)
    x_first, x_last, y_first, y_last, extra, turned = pl.pallas_call(
        face_kernel,
        out_shape=[face] * 4 + [
            jax.ShapeDtypeStruct((ACT_MAX, PACK - LANES, LANES), BF16),
            jax.ShapeDtypeStruct((VZ, VX, VY, CH), F32),
        ],
        in_specs=[SMEM] * 3 + [VMEM] * 2,
        out_specs=[VMEM] * 6,
        compiler_params=pltpu.CompilerParams(vmem_limit_bytes=56 << 20),
        name="faces",
    )(active, parent_owner, parent_slot, latent, norm_gain.reshape(1, CH))
    x_last = after(x_last, b0)
    x_low, x_high = shift(x_last, "gx", 1), shift(x_first, "gx", -1)
    a2, b2 = ringed(after(a1, x_low)), ringed(after(b1, x_high))
    y_first, y_last = after(y_first, a1, b1), after(y_last, a1, b1)
    y_first = jnp.concatenate([x_low[:, :1], y_first, x_high[:, :1]], axis=1).reshape(-1, CH)
    y_last = jnp.concatenate([x_low[:, -1:], y_last, x_high[:, -1:]], axis=1).reshape(-1, CH)
    y_low, y_high = shift(y_last, "gy", 1), shift(y_first, "gy", -1)

    a3, b3 = ringed(after(a2, y_low, y_high)), ringed(after(b2, y_low, y_high))
    extra = after(extra, a2, b2)
    hidden, query = pl.pallas_call(
        conv_kernel,
        out_shape=(
            jax.ShapeDtypeStruct((ROWS, CH), F32),
            jax.ShapeDtypeStruct((ACT_MAX, PACK, LANES), BF16),
        ),
        in_specs=[SMEM] + [VMEM] * 8 + [HBM] + [VMEM] * 2,
        out_specs=(VMEM, VMEM),
        scratch_shapes=[
            pltpu.VMEM((3, VZ, VX + 2, VY, CH), F32),
            pltpu.VMEM((27, CH, CH), BF16),
            pltpu.SemaphoreType.DMA((9,)),
        ],
        compiler_params=pltpu.CompilerParams(vmem_limit_bytes=56 << 20),
        cost_estimate=pl.CostEstimate(flops=2 * 27 * ROWS * CH * CH, bytes_accessed=5 << 20, transcendentals=ROWS * CH),
        name="conv",
    )(
        active, turned, x_low, x_high, y_low, y_high, norm_gain.reshape(1, CH),
        conv_bias.reshape(1, CH), attn_gain.reshape(1, CH), conv_weight, q_weight, extra,
    )

    def along(block, step):
        return move(block, lambda ring, line, core: (ring, line + step, core))

    here = lax.axis_index("gx").astype(jnp.int32).reshape(1)
    a4 = ringed(after(a3, query))
    query = after(query, a3)
    queries = [query, along(query, 1), along(query, 2), along(after(query, b3), 3)]
    kv_all = [a0, a1, a2, a3, a4, b0, b1, b2, b3]
    kv_all += [swapped(after(block, *queries)) for block in (a1, a2, a3)] + [swapped(a4)]
    kv_all += [swapped(after(block, *queries)) for block in (b1, b2, b3)]
    parts = pl.pallas_call(
        attend_kernel,
        out_shape=[jax.ShapeDtypeStruct((ACT_MAX, PACK, LANES), BF16)] * LINE,
        in_specs=[SMEM] + [VMEM] * LINE + [ANY] * ARRAYS,
        out_specs=[VMEM] * LINE,
        scratch_shapes=[
            pltpu.VMEM((LINE * ACT_MAX, PACK - LANES, LANES), jnp.int32),
            pltpu.SMEM((LINE * ACT_MAX, PACK - LANES, LANES), jnp.int32),
            pltpu.SMEM((PAIRS,), jnp.int32),
            pltpu.SMEM((LINE * ACT_MAX,), jnp.int32),
            pltpu.VMEM((PAIRS, TOK, 2 * CH), BF16),
            pltpu.VMEM((LINE * ACT_MAX, CH, CH), BF16),
            pltpu.VMEM((PAIRS, LANES, LANES), F32),
            pltpu.VMEM((PAIRS, 8, LANES), F32),
            pltpu.SemaphoreType.DMA((PAIRS,)),
            pltpu.SemaphoreType.DMA,
        ],
        compiler_params=pltpu.CompilerParams(vmem_limit_bytes=56 << 20),
        name="attend",
    )(here, *queries, *kv_all)

    merged = [parts[0]] + [along(parts[d], -d) for d in range(1, LINE)]
    out = pl.pallas_call(
        merge_kernel,
        out_shape=jax.ShapeDtypeStruct((ROWS, CH), F32),
        in_specs=[SMEM] + [VMEM] * (LINE + 2),
        out_specs=VMEM,
        scratch_shapes=[
            pltpu.VMEM((ACT_MAX, LANES, LANES), BF16),
            pltpu.VMEM((2, ROWS, LANES), F32),
        ],
        compiler_params=pltpu.CompilerParams(vmem_limit_bytes=8 << 20),
        name="merge",
    )(active, *merged, hidden, out_weight)
    return out.reshape(VZ, VX, VY, CH).transpose(1, 2, 0, 3)


def solution(mesh):
    placed = (
        P("gx", "gy", None, None),
        P("gx", "gy", None),
        P("gx", "gy", None, None),
        P("gx", "gy", None, None),
        P("gx", None, None),
        P(),
        P(),
        P(),
        P(),
        P(),
        P(),
    )
    return jax.shard_map(
        per_device, mesh=mesh, in_specs=placed, out_specs=P("gx", "gy", None, None), check_vma=False
    )
```

```python
import math

import jax
import jax.numpy as jnp
from jax import lax
from jax.experimental import pallas as pl
from jax.experimental.pallas import tpu as pltpu
from jax.sharding import PartitionSpec as P

CH = 256
HEADS = 8
HEAD_DIM = 32
EDGE = 4
VX, VY, VZ = 8, 8, 4
ROWS = VX * VY * VZ
WINDOWS = 4
ACT_MAX = 3
PARENTS = 4
TOK = 128
LANES = 128
PACK = 144
SLOTS = 4
CHIP = 2 * SLOTS
ARRAYS = 16
RING, LINE, CORES = 8, 4, 2
PAIRS = LINE * ACT_MAX * PARENTS
GROUP = 4
SCALE = math.log2(math.e) / math.sqrt(HEAD_DIM)
LOWEST = -3e38
F32 = jnp.float32
BF16 = jnp.bfloat16
VMEM = pl.BlockSpec(memory_space=pltpu.VMEM)
SMEM = pl.BlockSpec(memory_space=pltpu.SMEM)
ANY = pl.BlockSpec(memory_space=pl.ANY)
HBM = pl.BlockSpec(memory_space=pltpu.HBM)
NT = (((1,), (1,)), ((), ()))


def row_mask(act_ref):
    low = lax.broadcasted_iota(jnp.int32, (VY, CH), 0) < EDGE
    flags = [act_ref[w // 2, w % 2, 0].astype(F32) for w in range(WINDOWS)]
    halves = [jnp.where(low, flags[2 * b], flags[2 * b + 1]) for b in range(2)]
    return jnp.concatenate(
        [jnp.broadcast_to(half[None], (EDGE, VY, CH)) for half in halves], axis=0
    )


def rank(act_ref, w):
    place = jnp.int32(0)
    for before in range(w):
        place = place + act_ref[before // 2, before % 2, 0]
    return place


def placement():
    row = lax.broadcasted_iota(jnp.int32, (ROWS, LANES), 0)
    lane = lax.broadcasted_iota(jnp.int32, (ROWS, LANES), 1)
    query = (row >> 6) * 16 + ((row >> 3) & 3) * 4 + (row & 3)
    return query == (lane & 63), ((row >> 5) & 1) * 2 + ((row >> 2) & 1), lane


def table_kernel(act_ref, owner_ref, slot_ref, *refs):
    extra_ref = refs[-1]
    row = lax.broadcasted_iota(jnp.int32, (16, LANES), 0)
    lane = lax.broadcasted_iota(jnp.int32, (16, LANES), 1)
    for s in range(ACT_MAX):
        extra = jnp.full((16, LANES), -1.0, F32)
        for w in range(WINDOWS):
            here = (act_ref[w // 2, w % 2, 0] > 0) & (rank(act_ref, w) == s)
            for p in range(PARENTS):
                code = owner_ref[0, 0, w, p] * SLOTS + slot_ref[0, 0, w, p]
                code = jnp.where(here, code, -1).astype(F32)
                extra = jnp.where((row == 0) & (lane == p), jnp.maximum(extra, code), extra)
        extra_ref[s] = extra.astype(BF16)


def face_kernel(
    act_ref, latent_ref, gain_ref, xa_ref, xb_ref, ya_ref, yb_ref, turned_ref
):
    for z in range(VZ):
        for x in range(VX):
            turned_ref[z, x] = latent_ref[x, :, z, :]
    mask = row_mask(act_ref)
    gain = gain_ref[...].reshape(1, 1, CH)

    def normed(values, flags):
        scale = lax.rsqrt(jnp.mean(values * values, axis=-1, keepdims=True) + 1e-06)
        return (flags * values * scale * gain).astype(BF16)

    for side, ref in ((0, xa_ref), (VX - 1, xb_ref)):
        ref[...] = normed(turned_ref[:, side], mask[side][None])
    for side, ref in ((0, ya_ref), (VY - 1, yb_ref)):
        ref[...] = normed(turned_ref[:, :, side, :], mask[:, side, :][None])


def edge_kernel(xlo_ref, xhi_ref, ya_ref, yb_ref, outa_ref, outb_ref):
    for side, face_ref, out_ref in ((0, ya_ref, outa_ref), (VY - 1, yb_ref, outb_ref)):
        for z in range(VZ):
            low = xlo_ref[z].astype(F32)[side : side + 1]
            high = xhi_ref[z].astype(F32)[side : side + 1]
            line = jnp.concatenate([low, face_ref[z].astype(F32), high, jnp.zeros((6, CH), F32)], axis=0)
            out_ref[z] = line.astype(BF16)


def conv_kernel(
    act_ref, latent_ref, xlo_ref, xhi_ref, ylo_ref, yhi_ref, ngain_ref, bias_ref,
    again_ref, weight_ref, qw_ref, extra_ref, hidden_ref, query_ref,
    frame, weights, wide, sems,
):
    copies = [
        pltpu.make_async_copy(weight_ref.at[pl.ds(3 * ab, 3)], weights.at[:, ab], sems.at[ab])
        for ab in range(9)
    ]
    for copy in copies:
        copy.start()
    latent = latent_ref[...]
    mask = row_mask(act_ref)[None]
    scale = lax.rsqrt(jnp.mean(latent * latent, axis=-1, keepdims=True) + 1e-06)
    normed = mask * latent * scale * ngain_ref[...].reshape(1, 1, 1, CH)
    frame[1, :, 1 : VX + 1] = normed
    frame[1, :, 0] = xlo_ref[...].astype(F32)
    frame[1, :, VX + 1] = xhi_ref[...].astype(F32)
    ylo = ylo_ref[...].astype(F32)
    yhi = yhi_ref[...].astype(F32)
    first = lax.broadcasted_iota(jnp.int32, (VY, CH), 0) == 0
    last = lax.broadcasted_iota(jnp.int32, (VY, CH), 0) == VY - 1
    for z in range(VZ):
        for x in range(VX + 2):
            here = frame[1, z, x]
            frame[0, z, x] = jnp.where(first, ylo[z, x : x + 1, :], pltpu.roll(here, 1, 0))
            frame[2, z, x] = jnp.where(last, yhi[z, x : x + 1, :], pltpu.roll(here, VY - 1, 0))
    conv = []
    for a in range(3):
        for b in range(3):
            wide[:, CH * b : CH * b + CH] = frame[b, :, a : a + VX].reshape(ROWS, CH).astype(BF16)
            copies[3 * a + b].wait()
        rows = (slice(0, ROWS - 64), slice(0, ROWS), slice(64, ROWS))
        for c in range(3):
            weight = weights[c, 3 * a : 3 * a + 3].reshape(3 * CH, CH)
            part = jnp.dot(wide[rows[c], :], weight, preferred_element_type=F32)
            conv.append(part)
    up, mid, down = (conv[c] + conv[3 + c] + conv[6 + c] for c in range(3))
    gap = jnp.zeros((64, CH), F32)
    conv = mid + jnp.concatenate([gap, up], 0) + jnp.concatenate([down, gap], 0) + bias_ref[...]
    flat_mask = jnp.broadcast_to(mask, (VZ, VX, VY, CH)).reshape(ROWS, CH)
    hidden = latent.reshape(ROWS, CH) + flat_mask * (conv / (1.0 + jnp.exp(-conv)))
    hidden_ref[...] = hidden
    scale = lax.rsqrt(jnp.mean(hidden * hidden, axis=-1, keepdims=True) + 1e-06)
    query_in = (hidden * scale * again_ref[...]).astype(BF16)
    queries = jnp.dot(query_in, qw_ref[...], preferred_element_type=F32).T.astype(BF16)
    left = lax.broadcasted_iota(jnp.int32, (HEAD_DIM, LANES), 1) < 64
    query_ref[:, :LANES, :] = jnp.zeros((ACT_MAX, LANES, LANES), BF16)
    query_ref[:, LANES:, :] = extra_ref[...]
    fits, window, _ = placement()
    for w in range(WINDOWS):
        @pl.when(act_ref[w // 2, w % 2, 0] > 0)
        def _(w=w):
            place = jnp.where(fits & (window == w), 1.0, 0.0).astype(BF16)
            both = jnp.dot(queries, place, preferred_element_type=F32)
            packed = [
                jnp.where(left, both[64 * j : 64 * j + 32], both[64 * j + 32 : 64 * j + 64]) for j in range(4)
            ]
            query_ref[rank(act_ref, w), :LANES, :] = jnp.concatenate(packed, axis=0).astype(BF16)


def attend_kernel(here_ref, *refs):
    query_refs, kv_refs, out_refs = refs[:LINE], refs[LINE : LINE + ARRAYS], refs[LINE + ARRAYS : 2 * LINE + ARRAYS]
    codes, code_ref, list_ref, match_ref, held, blocks, values, levels, sems, code_sem = refs[2 * LINE + ARRAYS :]
    here = here_ref[0]
    ring, line, core = here >> 3, (here >> 1) & 3, here & 1
    for source in range(LINE):
        for s in range(ACT_MAX):
            codes[source * ACT_MAX + s] = query_refs[source][s, LANES:, :].astype(F32).astype(jnp.int32)
    listing = pltpu.make_async_copy(codes, code_ref, code_sem)
    listing.start()
    left = lax.broadcasted_iota(jnp.int32, (HEAD_DIM, LANES), 1) < 64
    none = jnp.zeros((64, LANES), BF16)
    for source in range(LINE):
        for s in range(ACT_MAX):
            w = source * ACT_MAX + s
            for j in range(4):
                pair = query_refs[source][s, 32 * j : 32 * j + 32, :].astype(F32)
                lanes = slice(LANES * (j % 2), LANES * (j % 2) + LANES)
                beside = slice(LANES * (1 - j % 2), LANES * (1 - j % 2) + LANES)
                blocks[w, 64 * j : 64 * j + 32, lanes] = jnp.where(left, pair, 0.0).astype(BF16)
                blocks[w, 64 * j + 32 : 64 * j + 64, lanes] = jnp.where(left, 0.0, pair).astype(BF16)
                blocks[w, 64 * j : 64 * j + 64, beside] = none
    listing.wait()

    def fetch(w, count):
        def parents(count):
            for p in range(PARENTS):
                code = code_ref[w, 0, p]
                owner = code >> 2
                mine = ((owner >> 1) & 3) == line
                ahead, owner_core, slot = ((owner >> 3) - ring) & 7, owner & 1, code & 3
                below = ahead > 4
                steps = jnp.where(below, RING - ahead, ahead)
                brought = (ahead == 0) | (ahead == 4) | (below == (core == 0))
                own = owner_core == core
                array = jnp.where(
                    brought,
                    jnp.where(own, steps, jnp.where(ahead == 4, 12, 5 + steps)),
                    jnp.where(own, 12 + steps, 8 + steps),
                )

                @pl.when(mine)
                def _(count=count, array=array, slot=slot):
                    list_ref[count] = w
                    for quarter in range(0, ARRAYS, 4):
                        @pl.when((array >> 2) == quarter // 4)
                        def _(quarter=quarter):
                            for k in range(quarter, quarter + 4):
                                @pl.when(array == k)
                                def _(k=k):
                                    pltpu.make_async_copy(kv_refs[k].at[slot], held.at[count], sems.at[count]).start()
                count = count + mine.astype(jnp.int32)
            return count

        after = lax.cond(code_ref[w, 0, 0] >= 0, parents, lambda count: count, count)
        match_ref[w] = after - count
        return after

    count = lax.fori_loop(0, LINE * ACT_MAX, fetch, jnp.int32(0))

    def attend(at, w):
        for g in range(2):
            half = slice(LANES * g, LANES * g + LANES)
            scores = jnp.dot(held[at, :, half], blocks[w, half, :], preferred_element_type=F32)
            peak = jnp.max(scores, axis=0, keepdims=True)
            lifted = jnp.exp2((scores - peak) * SCALE)
            total = jnp.sum(lifted, axis=0, keepdims=True)
            turned = held[at, :, CH + LANES * g : CH + LANES * g + LANES].T
            mixed = jnp.dot(turned, lifted.astype(BF16), preferred_element_type=F32)
            for jj in range(2):
                cut = slice(LANES * jj, LANES * jj + LANES)
                row = 64 * jj
                kept = jnp.where(left, mixed[row : row + 32, cut], mixed[row + 32 : row + 64, cut])
                j = 2 * g + jj
                values[at, 32 * j : 32 * j + 32, :] = kept
                levels[at, j : j + 1, :] = peak[:, cut] * SCALE
                levels[at, 4 + j : 5 + j, :] = total[:, cut]

    def group(i, carry):
        for u in range(GROUP):
            at = i * GROUP + u

            @pl.when(at < count)
            def _(at=at):
                pltpu.make_async_copy(kv_refs[0].at[0], held.at[at], sems.at[at]).wait()
        window = [list_ref[jnp.minimum(i * GROUP + u, count - 1)] for u in range(GROUP)]
        for u in range(GROUP):
            attend(i * GROUP + u, window[u])
        return carry

    lax.fori_loop(0, (count + GROUP - 1) // GROUP, group, 0)
    rows = lax.broadcasted_iota(jnp.int32, (PACK - LANES, LANES), 0)
    done = jnp.int32(0)
    for source in range(LINE):
        out_ref = out_refs[source]
        for s in range(ACT_MAX):
            w = source * ACT_MAX + s
            matches = match_ref[w]

            @pl.when(matches == 0)
            def _(s=s, out_ref=out_ref):
                out_ref[s, :LANES, :] = jnp.zeros((LANES, LANES), BF16)
                out_ref[s, LANES:, :] = jnp.where(rows < 4, LOWEST, 0.0).astype(BF16)

            @pl.when(matches > 0)
            def _(s=s, out_ref=out_ref, done=done, matches=matches):
                def join(k, state):
                    peak, total, value = state
                    new = jnp.maximum(peak, levels[done + k, 0:4, :])
                    fade, gain = jnp.exp2(peak - new), jnp.exp2(levels[done + k, 0:4, :] - new)
                    total = total * fade + levels[done + k, 4:8, :] * gain
                    value = jnp.concatenate(
                        [
                            value[32 * j : 32 * j + 32] * fade[j : j + 1]
                            + values[done + k, 32 * j : 32 * j + 32, :] * gain[j : j + 1]
                            for j in range(4)
                        ],
                        axis=0,
                    )
                    return new, total, value

                first = (levels[done, 0:4, :], levels[done, 4:8, :], values[done])
                peak, total, value = lax.fori_loop(1, matches, join, first)
                for j in range(4):
                    cut = slice(32 * j, 32 * j + 32)
                    out_ref[s, cut, :] = (value[cut] / total[j : j + 1]).astype(BF16)
                level = peak + jnp.log2(total)
                high = level.astype(BF16).astype(F32)
                middle = (level - high).astype(BF16).astype(F32)
                low = level - high - middle
                stats = jnp.concatenate([high, middle, low, jnp.zeros_like(low)], axis=0)
                out_ref[s, LANES:, :] = stats.astype(BF16)

            done = done + matches


def merge_kernel(act_ref, *refs):
    part_refs = refs[:LINE]
    hidden_ref, ow_ref, out_ref, mixed, attended = refs[LINE:]
    for s in range(ACT_MAX):
        stats = [ref[s, LANES:, :].astype(F32) for ref in part_refs]
        levels = [one[0:4] + one[4:8] + one[8:12] for one in stats]
        top = jnp.maximum(jnp.maximum(levels[0], levels[1]), jnp.maximum(levels[2], levels[3]))
        shares = [jnp.exp2(level - top) for level in levels]
        whole = shares[0] + shares[1] + shares[2] + shares[3]
        for j in range(4):
            rows = slice(32 * j, 32 * j + 32)
            value = jnp.zeros((HEAD_DIM, LANES), F32)
            for ref, share in zip(part_refs, shares):
                value = value + ref[s, rows, :].astype(F32) * (share / whole)[j : j + 1, :]
            mixed[s, rows, :] = value.astype(BF16)
    attended[...] = jnp.zeros_like(attended)
    fits, window, lane = placement()
    for w in range(WINDOWS):
        @pl.when(act_ref[w // 2, w % 2, 0] > 0)
        def _(w=w):
            block = mixed[rank(act_ref, w)]
            for side in range(2):
                place = jnp.where(fits & (window == w) & ((lane >> 6) == side), 1.0, 0.0).astype(BF16)
                attended[side] += lax.dot_general(place, block, NT, preferred_element_type=F32)
    projected = jnp.zeros((ROWS, CH), F32)
    for side in range(2):
        weight = jnp.concatenate([ow_ref[64 * j + 32 * side : 64 * j + 32 * side + 32, :] for j in range(4)], axis=0)
        projected = projected + jnp.dot(attended[side].astype(BF16), weight, preferred_element_type=F32)
    mask = jnp.broadcast_to(row_mask(act_ref)[None], (VZ, VX, VY, CH)).reshape(ROWS, CH)
    result = (mask * (hidden_ref[...] + projected)).reshape(VZ, VX, VY, CH)
    for z in range(VZ):
        for x in range(VX):
            out_ref[x, :, z, :] = result[z, x]


def shift(block, axis, step):
    count = lax.axis_size(axis)
    return lax.ppermute(block, axis, [(i, i + step) for i in range(count) if 0 <= i + step < count])


def after(block, *others):
    return lax.optimization_barrier((block, *others))[0]


def move(block, rule):
    pairs = []
    for i in range(RING * LINE * CORES):
        ring, line, core = rule(i // (LINE * CORES), i // CORES % LINE, i % CORES)
        pairs.append((i, (ring % RING * LINE + line % LINE) * CORES + core))
    return lax.ppermute(block, "gx", pairs)


def per_device(
    latent, active, parent_owner, parent_slot, coarse_kv, norm_gain, conv_weight, conv_bias,
    attn_gain, q_weight, out_weight,
):
    def swapped(block):
        return move(block, lambda ring, line, core: (ring, line, 1 - core))

    def ringed(block):
        return move(block, lambda ring, line, core: (ring + 1 - 2 * core, line, core))

    a0, a1, b0 = coarse_kv, ringed(coarse_kv), swapped(coarse_kv)

    face = jax.ShapeDtypeStruct((VZ, VX, CH), BF16)
    vectors = [one.reshape(1, CH) for one in (norm_gain, conv_bias, attn_gain)]
    extra = pl.pallas_call(
        table_kernel,
        out_shape=jax.ShapeDtypeStruct((ACT_MAX, PACK - LANES, LANES), BF16),
        in_specs=[SMEM] * 3 + [ANY] * 6,
        out_specs=VMEM,
        compiler_params=pltpu.CompilerParams(vmem_limit_bytes=60 << 20),
        name="tables",
    )(active, parent_owner, parent_slot, *vectors, conv_weight, q_weight, latent)
    vectors[0] = after(vectors[0], extra)
    x_first, x_last, y_first, y_last, turned = pl.pallas_call(
        face_kernel,
        out_shape=[face] * 4 + [
            jax.ShapeDtypeStruct((VZ, VX, VY, CH), F32),
        ],
        in_specs=[SMEM] + [VMEM] * 2,
        out_specs=[VMEM] * 5,
        compiler_params=pltpu.CompilerParams(vmem_limit_bytes=6 << 20),
        name="faces",
    )(active, latent, vectors[0])
    b1 = ringed(after(b0, x_first, x_last))
    x_low, x_high = shift(x_last, "gx", 1), shift(x_first, "gx", -1)
    a2, b2 = ringed(after(a1, x_low, x_high)), ringed(after(b1, x_low, x_high))
    y_first, y_last = after(y_first, a1, b1), after(y_last, a1, b1)
    y_first, y_last = pl.pallas_call(
        edge_kernel,
        out_shape=[jax.ShapeDtypeStruct((VZ, 16, CH), BF16)] * 2,
        in_specs=[VMEM] * 4,
        out_specs=[VMEM] * 2,
        compiler_params=pltpu.CompilerParams(vmem_limit_bytes=6 << 20),
        name="edges",
    )(x_low, x_high, y_first, y_last)
    y_low, y_high = shift(y_last, "gy", 1), shift(y_first, "gy", -1)

    a3 = ringed(after(a2, y_low, y_high))
    extra = after(extra, a2)
    hidden, query = pl.pallas_call(
        conv_kernel,
        out_shape=(
            jax.ShapeDtypeStruct((ROWS, CH), F32),
            jax.ShapeDtypeStruct((ACT_MAX, PACK, LANES), BF16),
        ),
        in_specs=[SMEM] + [VMEM] * 8 + [ANY] + [VMEM] * 2,
        out_specs=(VMEM, VMEM),
        scratch_shapes=[
            pltpu.VMEM((3, VZ, VX + 2, VY, CH), F32),
            pltpu.VMEM((3, 9, CH, CH), BF16),
            pltpu.VMEM((ROWS, 3 * CH), BF16),
            pltpu.SemaphoreType.DMA((9,)),
        ],
        compiler_params=pltpu.CompilerParams(vmem_limit_bytes=16 << 20),
        cost_estimate=pl.CostEstimate(flops=2 * 27 * ROWS * CH * CH, bytes_accessed=5 << 20, transcendentals=ROWS * CH),
        name="conv",
    )(
        active, turned, x_low, x_high, y_low, y_high, vectors[0],
        vectors[1], vectors[2], conv_weight, q_weight, extra,
    )

    def along(block, step):
        return move(block, lambda ring, line, core: (ring, line + step, core))

    here = lax.axis_index("gx").astype(jnp.int32).reshape(1)
    query = after(query, b2)
    b3 = ringed(after(b2, query))
    queries = [query] + [along(query, d) for d in range(1, LINE)]
    a4 = ringed(after(a3, query))
    xa1, xb1, xa2, xb2, xa3, xb3 = (swapped(after(block, *queries, b3)) for block in (a1, b1, a2, b2, a3, b3))
    xa4 = swapped(after(a4, *queries))
    kv_all = [a0, a1, a2, a3, a4, b0, b1, b2, b3, xa1, xa2, xa3, xa4, xb1, xb2, xb3]
    parts = pl.pallas_call(
        attend_kernel,
        out_shape=[jax.ShapeDtypeStruct((ACT_MAX, PACK, LANES), BF16)] * LINE,
        in_specs=[SMEM] + [VMEM] * LINE + [ANY] * ARRAYS,
        out_specs=[VMEM] * LINE,
        scratch_shapes=[
            pltpu.VMEM((LINE * ACT_MAX, PACK - LANES, LANES), jnp.int32),
            pltpu.SMEM((LINE * ACT_MAX, PACK - LANES, LANES), jnp.int32),
            pltpu.SMEM((PAIRS,), jnp.int32),
            pltpu.SMEM((LINE * ACT_MAX,), jnp.int32),
            pltpu.VMEM((PAIRS, TOK, 2 * CH), BF16),
            pltpu.VMEM((LINE * ACT_MAX, CH, CH), BF16),
            pltpu.VMEM((PAIRS, LANES, LANES), F32),
            pltpu.VMEM((PAIRS, 8, LANES), F32),
            pltpu.SemaphoreType.DMA((PAIRS,)),
            pltpu.SemaphoreType.DMA,
        ],
        compiler_params=pltpu.CompilerParams(vmem_limit_bytes=56 << 20),
        name="attend",
    )(here, *queries, *kv_all)

    merged = [parts[0]] + [along(parts[d], -d) for d in range(1, LINE)]
    return pl.pallas_call(
        merge_kernel,
        out_shape=jax.ShapeDtypeStruct((VX, VY, VZ, CH), F32),
        in_specs=[SMEM] + [VMEM] * (LINE + 2),
        out_specs=VMEM,
        scratch_shapes=[
            pltpu.VMEM((ACT_MAX, LANES, LANES), BF16),
            pltpu.VMEM((2, ROWS, LANES), F32),
        ],
        compiler_params=pltpu.CompilerParams(vmem_limit_bytes=8 << 20),
        name="merge",
    )(active, *merged, hidden, out_weight)


def solution(mesh):
    placed = (
        P("gx", "gy", None, None),
        P("gx", "gy", None),
        P("gx", "gy", None, None),
        P("gx", "gy", None, None),
        P("gx", None, None),
        P(),
        P(),
        P(),
        P(),
        P(),
        P(),
    )
    return jax.shard_map(
        per_device, mesh=mesh, in_specs=placed, out_specs=P("gx", "gy", None, None), check_vma=False
    )
```

```python
import math

import jax
import jax.numpy as jnp
from jax import lax
from jax.experimental import pallas as pl
from jax.experimental.pallas import tpu as pltpu
from jax.sharding import PartitionSpec as P

CH = 256
HEADS = 8
HEAD_DIM = 32
EDGE = 4
VX, VY, VZ = 8, 8, 4
ROWS = VX * VY * VZ
WINDOWS = 4
ACT_MAX = 3
PARENTS = 4
TOK = 128
LANES = 128
PACK = 144
SLOTS = 4
CHIP = 2 * SLOTS
ARRAYS = 16
RING, LINE, CORES = 8, 4, 2
PAIRS = LINE * ACT_MAX * PARENTS
GROUP = 4
SCALE = math.log2(math.e) / math.sqrt(HEAD_DIM)
LOWEST = -3e38
F32 = jnp.float32
BF16 = jnp.bfloat16
VMEM = pl.BlockSpec(memory_space=pltpu.VMEM)
SMEM = pl.BlockSpec(memory_space=pltpu.SMEM)
ANY = pl.BlockSpec(memory_space=pl.ANY)
HBM = pl.BlockSpec(memory_space=pltpu.HBM)
NT = (((1,), (1,)), ((), ()))


def row_mask(act_ref):
    low = lax.broadcasted_iota(jnp.int32, (VY, CH), 0) < EDGE
    flags = [act_ref[w // 2, w % 2, 0].astype(F32) for w in range(WINDOWS)]
    halves = [jnp.where(low, flags[2 * b], flags[2 * b + 1]) for b in range(2)]
    return jnp.concatenate(
        [jnp.broadcast_to(half[None], (EDGE, VY, CH)) for half in halves], axis=0
    )


def rank(act_ref, w):
    place = jnp.int32(0)
    for before in range(w):
        place = place + act_ref[before // 2, before % 2, 0]
    return place


def placement():
    row = lax.broadcasted_iota(jnp.int32, (ROWS, LANES), 0)
    lane = lax.broadcasted_iota(jnp.int32, (ROWS, LANES), 1)
    query = (row >> 6) * 16 + ((row >> 3) & 3) * 4 + (row & 3)
    return query == (lane & 63), ((row >> 5) & 1) * 2 + ((row >> 2) & 1), lane


def near_kernel(*refs):
    refs[-1][...] = jnp.zeros_like(refs[-1])


def face_kernel(
    act_ref, owner_ref, slot_ref, latent_ref, gain_ref, near_ref,
    xa_ref, xb_ref, ya_ref, yb_ref, turned_ref, extra_ref,
):
    for z in range(VZ):
        for x in range(VX):
            turned_ref[z, x] = latent_ref[x, :, z, :]
    mask = row_mask(act_ref)
    gain = gain_ref[...].reshape(1, 1, CH)

    def normed(values, flags):
        scale = lax.rsqrt(jnp.mean(values * values, axis=-1, keepdims=True) + 1e-06)
        return (flags * values * scale * gain).astype(BF16)

    for side, ref in ((0, xa_ref), (VX - 1, xb_ref)):
        ref[...] = normed(turned_ref[:, side], mask[side][None])
    for side, ref in ((0, ya_ref), (VY - 1, yb_ref)):
        ref[...] = normed(turned_ref[:, :, side, :], mask[:, side, :][None])
    row = lax.broadcasted_iota(jnp.int32, (16, LANES), 0)
    lane = lax.broadcasted_iota(jnp.int32, (16, LANES), 1)
    for s in range(ACT_MAX):
        extra = jnp.full((16, LANES), -1.0, F32)
        for w in range(WINDOWS):
            here = (act_ref[w // 2, w % 2, 0] > 0) & (rank(act_ref, w) == s)
            for p in range(PARENTS):
                code = owner_ref[0, 0, w, p] * SLOTS + slot_ref[0, 0, w, p]
                code = jnp.where(here, code, -1).astype(F32)
                extra = jnp.where((row == 0) & (lane == p), jnp.maximum(extra, code), extra)
        extra_ref[s] = extra.astype(BF16)


def edge_kernel(xlo_ref, xhi_ref, ya_ref, yb_ref, outa_ref, outb_ref):
    for side, face_ref, out_ref in ((0, ya_ref, outa_ref), (VY - 1, yb_ref, outb_ref)):
        for z in range(VZ):
            low = xlo_ref[z].astype(F32)[side : side + 1]
            high = xhi_ref[z].astype(F32)[side : side + 1]
            line = jnp.concatenate([low, face_ref[z].astype(F32), high, jnp.zeros((6, CH), F32)], axis=0)
            out_ref[z] = line.astype(BF16)


def conv_kernel(
    act_ref, latent_ref, xlo_ref, xhi_ref, ylo_ref, yhi_ref, ngain_ref, bias_ref,
    again_ref, weight_ref, qw_ref, extra_ref, hidden_ref, query_ref,
    frame, weights, wide, sems,
):
    copies = [
        pltpu.make_async_copy(weight_ref.at[pl.ds(3 * ab, 3)], weights.at[:, ab], sems.at[ab])
        for ab in range(9)
    ]
    for copy in copies:
        copy.start()
    latent = latent_ref[...]
    mask = row_mask(act_ref)[None]
    scale = lax.rsqrt(jnp.mean(latent * latent, axis=-1, keepdims=True) + 1e-06)
    normed = mask * latent * scale * ngain_ref[...].reshape(1, 1, 1, CH)
    frame[1, :, 1 : VX + 1] = normed
    frame[1, :, 0] = xlo_ref[...].astype(F32)
    frame[1, :, VX + 1] = xhi_ref[...].astype(F32)
    ylo = ylo_ref[...].astype(F32)
    yhi = yhi_ref[...].astype(F32)
    first = lax.broadcasted_iota(jnp.int32, (VY, CH), 0) == 0
    last = lax.broadcasted_iota(jnp.int32, (VY, CH), 0) == VY - 1
    for z in range(VZ):
        for x in range(VX + 2):
            here = frame[1, z, x]
            frame[0, z, x] = jnp.where(first, ylo[z, x : x + 1, :], pltpu.roll(here, 1, 0))
            frame[2, z, x] = jnp.where(last, yhi[z, x : x + 1, :], pltpu.roll(here, VY - 1, 0))
    conv = []
    for a in range(3):
        for b in range(3):
            wide[:, CH * b : CH * b + CH] = frame[b, :, a : a + VX].reshape(ROWS, CH).astype(BF16)
            copies[3 * a + b].wait()
        rows = (slice(0, ROWS - 64), slice(0, ROWS), slice(64, ROWS))
        for c in range(3):
            weight = weights[c, 3 * a : 3 * a + 3].reshape(3 * CH, CH)
            part = jnp.dot(wide[rows[c], :], weight, preferred_element_type=F32)
            conv.append(part)
    up, mid, down = (conv[c] + conv[3 + c] + conv[6 + c] for c in range(3))
    gap = jnp.zeros((64, CH), F32)
    conv = mid + jnp.concatenate([gap, up], 0) + jnp.concatenate([down, gap], 0) + bias_ref[...]
    flat_mask = jnp.broadcast_to(mask, (VZ, VX, VY, CH)).reshape(ROWS, CH)
    hidden = latent.reshape(ROWS, CH) + flat_mask * (conv / (1.0 + jnp.exp(-conv)))
    hidden_ref[...] = hidden
    scale = lax.rsqrt(jnp.mean(hidden * hidden, axis=-1, keepdims=True) + 1e-06)
    query_in = (hidden * scale * again_ref[...]).astype(BF16)
    queries = jnp.dot(query_in, qw_ref[...], preferred_element_type=F32).T.astype(BF16)
    left = lax.broadcasted_iota(jnp.int32, (HEAD_DIM, LANES), 1) < 64
    query_ref[:, :LANES, :] = jnp.zeros((ACT_MAX, LANES, LANES), BF16)
    query_ref[:, LANES:, :] = extra_ref[...]
    fits, window, _ = placement()
    for w in range(WINDOWS):
        @pl.when(act_ref[w // 2, w % 2, 0] > 0)
        def _(w=w):
            place = jnp.where(fits & (window == w), 1.0, 0.0).astype(BF16)
            both = jnp.dot(queries, place, preferred_element_type=F32)
            packed = [
                jnp.where(left, both[64 * j : 64 * j + 32], both[64 * j + 32 : 64 * j + 64]) for j in range(4)
            ]
            query_ref[rank(act_ref, w), :LANES, :] = jnp.concatenate(packed, axis=0).astype(BF16)


def attend_kernel(here_ref, *refs):
    query_refs, kv_refs, out_refs = refs[:LINE], refs[LINE : LINE + ARRAYS], refs[LINE + ARRAYS : 2 * LINE + ARRAYS]
    codes, code_ref, list_ref, match_ref, held, blocks, values, levels, sems, code_sem = refs[2 * LINE + ARRAYS :]
    here = here_ref[0]
    ring, line, core = here >> 3, (here >> 1) & 3, here & 1
    for source in range(LINE):
        for s in range(ACT_MAX):
            codes[source * ACT_MAX + s] = query_refs[source][s, LANES:, :].astype(F32).astype(jnp.int32)
    listing = pltpu.make_async_copy(codes, code_ref, code_sem)
    listing.start()
    left = lax.broadcasted_iota(jnp.int32, (HEAD_DIM, LANES), 1) < 64
    none = jnp.zeros((64, LANES), BF16)
    for source in range(LINE):
        for s in range(ACT_MAX):
            w = source * ACT_MAX + s
            for j in range(4):
                pair = query_refs[source][s, 32 * j : 32 * j + 32, :].astype(F32)
                lanes = slice(LANES * (j % 2), LANES * (j % 2) + LANES)
                beside = slice(LANES * (1 - j % 2), LANES * (1 - j % 2) + LANES)
                blocks[w, 64 * j : 64 * j + 32, lanes] = jnp.where(left, pair, 0.0).astype(BF16)
                blocks[w, 64 * j + 32 : 64 * j + 64, lanes] = jnp.where(left, 0.0, pair).astype(BF16)
                blocks[w, 64 * j : 64 * j + 64, beside] = none
    listing.wait()

    def fetch(w, count):
        def parents(count):
            for p in range(PARENTS):
                code = code_ref[w, 0, p]
                owner = code >> 2
                mine = ((owner >> 1) & 3) == line
                ahead, owner_core, slot = ((owner >> 3) - ring) & 7, owner & 1, code & 3
                below = ahead > 4
                steps = jnp.where(below, RING - ahead, ahead)
                brought = (ahead == 0) | (ahead == 4) | (below == (core == 0))
                own = owner_core == core
                array = jnp.where(
                    brought,
                    jnp.where(own, steps, jnp.where(ahead == 4, 12, 5 + steps)),
                    jnp.where(own, 12 + steps, 8 + steps),
                )

                @pl.when(mine)
                def _(count=count, array=array, slot=slot):
                    list_ref[count] = w
                    for quarter in range(0, ARRAYS, 4):
                        @pl.when((array >> 2) == quarter // 4)
                        def _(quarter=quarter):
                            for k in range(quarter, quarter + 4):
                                @pl.when(array == k)
                                def _(k=k):
                                    pltpu.make_async_copy(kv_refs[k].at[slot], held.at[count], sems.at[count]).start()
                count = count + mine.astype(jnp.int32)
            return count

        after = lax.cond(code_ref[w, 0, 0] >= 0, parents, lambda count: count, count)
        match_ref[w] = after - count
        return after

    count = lax.fori_loop(0, LINE * ACT_MAX, fetch, jnp.int32(0))

    def attend(at, w):
        for g in range(2):
            half = slice(LANES * g, LANES * g + LANES)
            scores = jnp.dot(held[at, :, half], blocks[w, half, :], preferred_element_type=F32)
            peak = jnp.max(scores, axis=0, keepdims=True)
            lifted = jnp.exp2((scores - peak) * SCALE)
            total = jnp.sum(lifted, axis=0, keepdims=True)
            turned = held[at, :, CH + LANES * g : CH + LANES * g + LANES].T
            mixed = jnp.dot(turned, lifted.astype(BF16), preferred_element_type=F32)
            for jj in range(2):
                cut = slice(LANES * jj, LANES * jj + LANES)
                row = 64 * jj
                kept = jnp.where(left, mixed[row : row + 32, cut], mixed[row + 32 : row + 64, cut])
                j = 2 * g + jj
                values[at, 32 * j : 32 * j + 32, :] = kept
                levels[at, j : j + 1, :] = peak[:, cut] * SCALE
                levels[at, 4 + j : 5 + j, :] = total[:, cut]

    def group(i, carry):
        for u in range(GROUP):
            at = i * GROUP + u

            @pl.when(at < count)
            def _(at=at):
                pltpu.make_async_copy(kv_refs[0].at[0], held.at[at], sems.at[at]).wait()
        window = [list_ref[jnp.minimum(i * GROUP + u, count - 1)] for u in range(GROUP)]
        for u in range(GROUP):
            attend(i * GROUP + u, window[u])
        return carry

    lax.fori_loop(0, (count + GROUP - 1) // GROUP, group, 0)
    rows = lax.broadcasted_iota(jnp.int32, (PACK - LANES, LANES), 0)
    done = jnp.int32(0)
    for source in range(LINE):
        out_ref = out_refs[source]
        for s in range(ACT_MAX):
            w = source * ACT_MAX + s
            matches = match_ref[w]

            @pl.when(matches == 0)
            def _(s=s, out_ref=out_ref):
                out_ref[s, :LANES, :] = jnp.zeros((LANES, LANES), BF16)
                out_ref[s, LANES:, :] = jnp.where(rows < 4, LOWEST, 0.0).astype(BF16)

            @pl.when(matches > 0)
            def _(s=s, out_ref=out_ref, done=done, matches=matches):
                def join(k, state):
                    peak, total, value = state
                    new = jnp.maximum(peak, levels[done + k, 0:4, :])
                    fade, gain = jnp.exp2(peak - new), jnp.exp2(levels[done + k, 0:4, :] - new)
                    total = total * fade + levels[done + k, 4:8, :] * gain
                    value = jnp.concatenate(
                        [
                            value[32 * j : 32 * j + 32] * fade[j : j + 1]
                            + values[done + k, 32 * j : 32 * j + 32, :] * gain[j : j + 1]
                            for j in range(4)
                        ],
                        axis=0,
                    )
                    return new, total, value

                first = (levels[done, 0:4, :], levels[done, 4:8, :], values[done])
                peak, total, value = lax.fori_loop(1, matches, join, first)
                for j in range(4):
                    cut = slice(32 * j, 32 * j + 32)
                    out_ref[s, cut, :] = (value[cut] / total[j : j + 1]).astype(BF16)
                level = peak + jnp.log2(total)
                high = level.astype(BF16).astype(F32)
                middle = (level - high).astype(BF16).astype(F32)
                low = level - high - middle
                stats = jnp.concatenate([high, middle, low, jnp.zeros_like(low)], axis=0)
                out_ref[s, LANES:, :] = stats.astype(BF16)

            done = done + matches


def merge_kernel(act_ref, *refs):
    part_refs = refs[:LINE]
    hidden_ref, ow_ref, out_ref, mixed, attended = refs[LINE:]
    for s in range(ACT_MAX):
        stats = [ref[s, LANES:, :].astype(F32) for ref in part_refs]
        levels = [one[0:4] + one[4:8] + one[8:12] for one in stats]
        top = jnp.maximum(jnp.maximum(levels[0], levels[1]), jnp.maximum(levels[2], levels[3]))
        shares = [jnp.exp2(level - top) for level in levels]
        whole = shares[0] + shares[1] + shares[2] + shares[3]
        for j in range(4):
            rows = slice(32 * j, 32 * j + 32)
            value = jnp.zeros((HEAD_DIM, LANES), F32)
            for ref, share in zip(part_refs, shares):
                value = value + ref[s, rows, :].astype(F32) * (share / whole)[j : j + 1, :]
            mixed[s, rows, :] = value.astype(BF16)
    attended[...] = jnp.zeros_like(attended)
    fits, window, lane = placement()
    for w in range(WINDOWS):
        @pl.when(act_ref[w // 2, w % 2, 0] > 0)
        def _(w=w):
            block = mixed[rank(act_ref, w)]
            for side in range(2):
                place = jnp.where(fits & (window == w) & ((lane >> 6) == side), 1.0, 0.0).astype(BF16)
                attended[side] += lax.dot_general(place, block, NT, preferred_element_type=F32)
    projected = jnp.zeros((ROWS, CH), F32)
    for side in range(2):
        weight = jnp.concatenate([ow_ref[64 * j + 32 * side : 64 * j + 32 * side + 32, :] for j in range(4)], axis=0)
        projected = projected + jnp.dot(attended[side].astype(BF16), weight, preferred_element_type=F32)
    mask = jnp.broadcast_to(row_mask(act_ref)[None], (VZ, VX, VY, CH)).reshape(ROWS, CH)
    result = (mask * (hidden_ref[...] + projected)).reshape(VZ, VX, VY, CH)
    for z in range(VZ):
        for x in range(VX):
            out_ref[x, :, z, :] = result[z, x]


def shift(block, axis, step):
    count = lax.axis_size(axis)
    return lax.ppermute(block, axis, [(i, i + step) for i in range(count) if 0 <= i + step < count])


def after(block, *others):
    return lax.optimization_barrier((block, *others))[0]


def move(block, rule):
    pairs = []
    for i in range(RING * LINE * CORES):
        ring, line, core = rule(i // (LINE * CORES), i // CORES % LINE, i % CORES)
        pairs.append((i, (ring % RING * LINE + line % LINE) * CORES + core))
    return lax.ppermute(block, "gx", pairs)


def per_device(
    latent, active, parent_owner, parent_slot, coarse_kv, norm_gain, conv_weight, conv_bias,
    attn_gain, q_weight, out_weight,
):
    def swapped(block):
        return move(block, lambda ring, line, core: (ring, line, 1 - core))

    def ringed(block):
        return move(block, lambda ring, line, core: (ring + 1 - 2 * core, line, core))

    a0, a1, b0 = coarse_kv, ringed(coarse_kv), swapped(coarse_kv)

    face = jax.ShapeDtypeStruct((VZ, VX, CH), BF16)
    vectors = [one.reshape(1, CH) for one in (norm_gain, conv_bias, attn_gain)]
    near = pl.pallas_call(
        near_kernel,
        out_shape=jax.ShapeDtypeStruct((8, LANES), F32),
        in_specs=[ANY] * 6,
        out_specs=VMEM,
        compiler_params=pltpu.CompilerParams(vmem_limit_bytes=60 << 20),
        name="near",
    )(*vectors, conv_weight, q_weight, latent)
    x_first, x_last, y_first, y_last, turned, extra = pl.pallas_call(
        face_kernel,
        out_shape=[face] * 4 + [
            jax.ShapeDtypeStruct((VZ, VX, VY, CH), F32),
            jax.ShapeDtypeStruct((ACT_MAX, PACK - LANES, LANES), BF16),
        ],
        in_specs=[SMEM] * 3 + [VMEM] * 2 + [ANY],
        out_specs=[VMEM] * 6,
        compiler_params=pltpu.CompilerParams(vmem_limit_bytes=6 << 20),
        name="faces",
    )(active, parent_owner, parent_slot, latent, vectors[0], near)
    b1 = ringed(after(b0, x_first, x_last))
    x_low, x_high = shift(x_last, "gx", 1), shift(x_first, "gx", -1)
    a2, b2 = ringed(after(a1, x_low, x_high)), ringed(after(b1, x_low, x_high))
    y_first, y_last = after(y_first, a1, b1), after(y_last, a1, b1)
    y_first, y_last = pl.pallas_call(
        edge_kernel,
        out_shape=[jax.ShapeDtypeStruct((VZ, 16, CH), BF16)] * 2,
        in_specs=[VMEM] * 4,
        out_specs=[VMEM] * 2,
        compiler_params=pltpu.CompilerParams(vmem_limit_bytes=6 << 20),
        name="edges",
    )(x_low, x_high, y_first, y_last)
    y_low, y_high = shift(y_last, "gy", 1), shift(y_first, "gy", -1)

    a3 = ringed(after(a2, y_low, y_high))
    extra = after(extra, a2)
    hidden, query = pl.pallas_call(
        conv_kernel,
        out_shape=(
            jax.ShapeDtypeStruct((ROWS, CH), F32),
            jax.ShapeDtypeStruct((ACT_MAX, PACK, LANES), BF16),
        ),
        in_specs=[SMEM] + [VMEM] * 8 + [ANY] + [VMEM] * 2,
        out_specs=(VMEM, VMEM),
        scratch_shapes=[
            pltpu.VMEM((3, VZ, VX + 2, VY, CH), F32),
            pltpu.VMEM((3, 9, CH, CH), BF16),
            pltpu.VMEM((ROWS, 3 * CH), BF16),
            pltpu.SemaphoreType.DMA((9,)),
        ],
        compiler_params=pltpu.CompilerParams(vmem_limit_bytes=16 << 20),
        cost_estimate=pl.CostEstimate(flops=2 * 27 * ROWS * CH * CH, bytes_accessed=5 << 20, transcendentals=ROWS * CH),
        name="conv",
    )(
        active, turned, x_low, x_high, y_low, y_high, vectors[0],
        vectors[1], vectors[2], conv_weight, q_weight, extra,
    )

    def along(block, step):
        return move(block, lambda ring, line, core: (ring, line + step, core))

    here = lax.axis_index("gx").astype(jnp.int32).reshape(1)
    query = after(query, b2)
    b3 = ringed(after(b2, query))
    queries = [query] + [along(query, d) for d in range(1, LINE)]
    a4 = ringed(after(a3, query))
    xa1, xb1, xa2, xb2, xa3, xb3 = (swapped(after(block, *queries, b3)) for block in (a1, b1, a2, b2, a3, b3))
    xa4 = swapped(after(a4, *queries))
    kv_all = [a0, a1, a2, a3, a4, b0, b1, b2, b3, xa1, xa2, xa3, xa4, xb1, xb2, xb3]
    parts = pl.pallas_call(
        attend_kernel,
        out_shape=[jax.ShapeDtypeStruct((ACT_MAX, PACK, LANES), BF16)] * LINE,
        in_specs=[SMEM] + [VMEM] * LINE + [ANY] * ARRAYS,
        out_specs=[VMEM] * LINE,
        scratch_shapes=[
            pltpu.VMEM((LINE * ACT_MAX, PACK - LANES, LANES), jnp.int32),
            pltpu.SMEM((LINE * ACT_MAX, PACK - LANES, LANES), jnp.int32),
            pltpu.SMEM((PAIRS,), jnp.int32),
            pltpu.SMEM((LINE * ACT_MAX,), jnp.int32),
            pltpu.VMEM((PAIRS, TOK, 2 * CH), BF16),
            pltpu.VMEM((LINE * ACT_MAX, CH, CH), BF16),
            pltpu.VMEM((PAIRS, LANES, LANES), F32),
            pltpu.VMEM((PAIRS, 8, LANES), F32),
            pltpu.SemaphoreType.DMA((PAIRS,)),
            pltpu.SemaphoreType.DMA,
        ],
        compiler_params=pltpu.CompilerParams(vmem_limit_bytes=56 << 20),
        name="attend",
    )(here, *queries, *kv_all)

    merged = [parts[0]] + [along(parts[d], -d) for d in range(1, LINE)]
    return pl.pallas_call(
        merge_kernel,
        out_shape=jax.ShapeDtypeStruct((VX, VY, VZ, CH), F32),
        in_specs=[SMEM] + [VMEM] * (LINE + 2),
        out_specs=VMEM,
        scratch_shapes=[
            pltpu.VMEM((ACT_MAX, LANES, LANES), BF16),
            pltpu.VMEM((2, ROWS, LANES), F32),
        ],
        compiler_params=pltpu.CompilerParams(vmem_limit_bytes=8 << 20),
        name="merge",
    )(active, *merged, hidden, out_weight)


def solution(mesh):
    placed = (
        P("gx", "gy", None, None),
        P("gx", "gy", None),
        P("gx", "gy", None, None),
        P("gx", "gy", None, None),
        P("gx", None, None),
        P(),
        P(),
        P(),
        P(),
        P(),
        P(),
    )
    return jax.shard_map(
        per_device, mesh=mesh, in_specs=placed, out_specs=P("gx", "gy", None, None), check_vma=False
    )
```
